128 devices in a mesh: section: 2 (over x_hi), fsdp: 32 (over y, z, x_lo), ctx: 2 (over core).
Axes of the slice: x: 4 (x_hi: 2, x_lo: 2; x = x_hi * 2 + x_lo), y: 4, z: 4, core: 2. Of those that a mesh axis runs over, the one named last changes fastest.
Arguments:
- tokens: bfloat16 [2, 4096, 960], P(None, ('fsdp', 'ctx')), may hold values from -6 to 6
- segments: int32 [2, 4096], P(None, 'fsdp'), may hold values from 0 to 4, as said below
- gain_attn: bfloat16 [2, 960], P('section', 'fsdp'), may hold values from 0.5 to 1.5
- w_qkv: bfloat16 [2, 960, 1600], P('section', 'fsdp'), may hold values from -0.1875 to 0.1875
- w_out: bfloat16 [2, 960, 960], P('section', 'fsdp'), may hold values from -0.75 to 0.75
- gain_ffn: bfloat16 [2, 960], P('section', 'fsdp'), may hold values from 0.5 to 1.5
- w_gu: bfloat16 [2, 960, 5120], P('section', 'fsdp'), may hold values from -0.1875 to 0.1875
- w_down: bfloat16 [2, 960, 2560], P('section', 'fsdp'), may hold values from -0.25 to 0.25
- d_out: bfloat16 [2, 4096, 960], P(None, ('fsdp', 'ctx')), may hold values from -6 to 6
Outputs:
- acts: bfloat16 [2, 2, 4096, 960], P('section', None, ('fsdp', 'ctx'))
- input_grad: bfloat16 [2, 2, 4096, 960], P('section', None, ('fsdp', 'ctx'))
- grad_gain_attn: float32 [2, 960], P('section', 'fsdp')
- grad_qkv: float32 [2, 960, 1600], P('section', 'fsdp')
- grad_out: float32 [2, 960, 960], P('section', 'fsdp')
- grad_gain_ffn: float32 [2, 960], P('section', 'fsdp')
- grad_gu: float32 [2, 960, 5120], P('section', 'fsdp')
- grad_down: float32 [2, 960, 2560], P('section', 'fsdp')
The draws below stay inside these ranges and needn't reach their ends.
Inputs may be any that keep to these rules, and one draw needn't show every extreme that they name: `segments`: within each sequence of 128 tokens the segment numbers start at 0, never fall, and end at 4.
All inputs are finite; a program needn't handle non-finite values.
Results may differ from the reference program's by a relative error of at most 0.034.
Values may be sent and summed in bfloat16 or wider, within the bound.
A program may use at most 256 MiB of HBM per device.

```python
import math
import jax
import jax.numpy as jnp
from jax import lax

D = 960
HEADS = 15
KV_HEADS = 5
HEAD = 64
FF = 2560
SEQ_LEN = 128
MICRO = 2
TOKENS = 4096
N_FSDP = 32


def draw_segments(key, part):
    key = jax.random.fold_in(key, 11)
    places = jnp.arange(SEQ_LEN, dtype=jnp.int32)
    quarter = SEQ_LEN // 4
    raw_scores = jax.random.randint(key, (MICRO, N_FSDP, SEQ_LEN), 0, 65536)
    scores = raw_scores * SEQ_LEN + places
    early = (places > 0) & (places < quarter)
    late = places > 3 * quarter
    first_vals, first_idx = lax.top_k(jnp.where(early, scores, -1), 2)
    last_vals, last_idx = lax.top_k(jnp.where(late, scores, -1), 2)
    chosen = jnp.concatenate([first_idx, last_idx], axis=2).astype(jnp.int32)
    numbers = jnp.sum((chosen[:, :, None, :] <= places[:, None]).astype(jnp.int32), axis=-1)
    return numbers.astype(jnp.int32).reshape(MICRO, N_FSDP * SEQ_LEN)


def levels(rng, extent, cuts, least, high):
    gain, own = 1.0, jax.random.fold_in(rng, 6)
    for axis_at, blocks in cuts:
        steps = jnp.exp(jax.random.uniform(jax.random.fold_in(own, axis_at), (blocks,), jnp.float32, least / len(cuts), high / len(cuts)))
        gain = gain * jnp.repeat(steps, extent[axis_at] // blocks).reshape([-1 if axis == axis_at else 1 for axis in range(len(extent))])
    return gain


def normal_values(key, extent, spread, bound, split=(), kind=jnp.bfloat16):
    values = jax.random.normal(key, extent, jnp.float32) * spread
    if len(split) > 0:
        values = levels(key, extent, split, -0.22, 0.18) * values
    return jnp.clip(values, min=-bound, max=bound).astype(kind)


def setup_inputs(seed: int = 0) -> dict:
    key_of = jax.random.split(jax.random.key(seed), 10)
    tokens = normal_values(key_of[0], (MICRO, TOKENS, D), 1.0, 6.0, ((1, 64),))
    segments = draw_segments(jax.random.fold_in(key_of[9], 71), 0)
    gain_attn = jnp.clip(1.0 + 0.1 * jax.random.normal(key_of[2], (2, D), jnp.float32), 0.5, 1.5).astype(jnp.bfloat16)
    w_qkv = normal_values(key_of[3], (2, D, HEADS * HEAD + 2 * KV_HEADS * HEAD), D ** -0.5, 0.1875, ((0, 2), (1, 32)))
    w_out = normal_values(key_of[4], (2, D, HEADS * HEAD), (HEADS * HEAD // 16) ** -0.5, 0.75, ((0, 2), (1, 32)))
    gain_ffn = jnp.clip(1.0 + 0.1 * jax.random.normal(key_of[5], (2, D), jnp.float32), 0.5, 1.5).astype(jnp.bfloat16)
    w_gu = normal_values(key_of[6], (2, D, 2 * FF), D ** -0.5, 0.1875, ((0, 2), (1, 32)))
    w_down = normal_values(key_of[7], (2, D, FF), (FF // 4) ** -0.5, 0.25, ((0, 2), (1, 32)))
    d_out = normal_values(key_of[8], (MICRO, TOKENS, D), 1.0, 6.0, ((1, 64),))
    return dict(tokens=tokens, segments=segments, gain_attn=gain_attn, w_qkv=w_qkv, w_out=w_out, gain_ffn=gain_ffn, w_gu=w_gu, w_down=w_down, d_out=d_out)


norm_eps = 1e-05
rope_base = 100000.0

@jax.custom_vjp
def low(v):
    return lax.optimization_barrier(v.astype(jnp.bfloat16)).astype(jnp.float32)

@jax.custom_vjp
def low_back(v):
    return v

def low_keep(v):
    return (low(v), None)

def low_pass(kept, grad):
    return (grad,)

def back_keep(v):
    return (v, None)

def back_low(kept, grad):
    return (low(grad),)
low.defvjp(low_keep, low_pass)
low_back.defvjp(back_keep, back_low)

def frequencies():
    return jnp.power(jnp.float32(rope_base), -jnp.arange(HEAD // 2, dtype=jnp.float32) * (2.0 / HEAD))

def rotate(vector, cosine, sine_part):
    half_width = vector.shape[-1] // 2
    first_half, second_half = (vector[..., :half_width], vector[..., half_width:])
    return jnp.concatenate([first_half * cosine - second_half * sine_part, second_half * cosine + first_half * sine_part], axis=-1)

def normalize(values):
    return values * lax.rsqrt(lax.optimization_barrier(jnp.mean(values * values, axis=-1, keepdims=True)) + norm_eps)

def layer(inputs, seg_rows, params):
    gain_one, weight_qkv, weight_out, gain_two, weight_gu, weight_down = params
    highest = lax.Precision.HIGHEST
    batch_size, length = (inputs.shape[0], inputs.shape[1])
    group_size = HEADS // KV_HEADS
    query_width = HEADS * HEAD
    kv_width = KV_HEADS * HEAD
    earlier = lax.optimization_barrier(jnp.sum((seg_rows[:, None, :] < seg_rows[:, :, None]).astype(jnp.int32), axis=2))
    position = jnp.arange(length, dtype=jnp.int32)[None, :] - earlier
    angles = position.astype(jnp.float32)[..., None] * frequencies()
    cosine, sine_part = (jnp.cos(angles), jnp.sin(angles))
    places = jnp.arange(length, dtype=jnp.int32)
    allowed = (seg_rows[:, :, None] == seg_rows[:, None, :]) & (places[None, None, :] <= places[None, :, None])
    normed = low(normalize(inputs) * gain_one)
    qkv = low_back(jnp.einsum('bld,de->ble', normed, weight_qkv, precision=highest))
    query_rows = low(rotate(qkv[..., :query_width].reshape(batch_size, length, KV_HEADS, group_size, HEAD), cosine[:, :, None, None, :], sine_part[:, :, None, None, :]))
    keys_all = low(rotate(qkv[..., query_width:query_width + kv_width].reshape(batch_size, length, KV_HEADS, HEAD), cosine[:, :, None, :], sine_part[:, :, None, :]))
    values_all = low(qkv[..., query_width + kv_width:].reshape(batch_size, length, KV_HEADS, HEAD))
    scores = low_back(jnp.einsum('bqgrd,bkgd->bgrqk', query_rows, keys_all, precision=highest) * HEAD ** (-0.5))
    scores = jnp.where(allowed[:, None, None], scores, -1e+30)
    row_peak = lax.optimization_barrier(jnp.max(scores, axis=-1, keepdims=True))
    exponent = jnp.exp(scores - row_peak)
    reduced_probabilities = low(exponent / lax.optimization_barrier(jnp.sum(exponent, axis=-1, keepdims=True)))
    attended = low(low_back(jnp.einsum('bgrqk,bkgd->bqgrd', reduced_probabilities, values_all, precision=highest)))
    attended = attended.reshape(batch_size, length, query_width)
    branch = low_back(jnp.einsum('ble,de->bld', attended, weight_out, precision=highest))
    hidden = inputs + branch
    normed_two = low(normalize(hidden) * gain_two)
    gate_up = low_back(jnp.einsum('bld,df->blf', normed_two, weight_gu, precision=highest))
    half_width = gate_up.shape[-1] // 2
    mixed = low(jax.nn.silu(gate_up[..., :half_width]) * gate_up[..., half_width:])
    result = low_back(jnp.einsum('blf,df->bld', mixed, weight_down, precision=highest))
    return hidden + result

def reference(tokens, segments, gain_attn, w_qkv, w_out, gain_ffn, w_gu, w_down, d_out):
    seq_total = tokens.shape[0] * tokens.shape[1] // SEQ_LEN
    group_seqs = math.gcd(seq_total, max(1, 4096 // SEQ_LEN))
    steps_count = seq_total // group_seqs

    def regroup(array):
        return array.reshape((steps_count, group_seqs, SEQ_LEN) + array.shape[2:])
    weights_all = (gain_attn, w_qkv, w_out, gain_ffn, w_gu, w_down)
    section_params = [tuple((weight[level].astype(jnp.float32) for weight in weights_all)) for level in range(2)]

    def one_group(summed, item):
        inputs, seg_rows, cotangent = item

        def apply_layer(values, params):
            return layer(values, seg_rows, params)
        out_first, back_first = jax.vjp(apply_layer, inputs.astype(jnp.float32), section_params[0])
        middle = low(out_first)
        out_second, back_second = jax.vjp(apply_layer, middle, section_params[1])
        d_middle, grads_second = back_second(cotangent.astype(jnp.float32))
        d_middle = low(d_middle)
        d_inputs, grads_first = back_first(d_middle)
        summed = jax.tree.map(lambda left, right: left + right, summed, (grads_first, grads_second))
        return (summed, (middle, low(out_second), d_inputs, d_middle))
    start_sums = jax.tree.map(jnp.zeros_like, (section_params[0], section_params[1]))
    summed, (middle, final, d_inputs, d_middle) = lax.scan(one_group, start_sums, (regroup(tokens), regroup(segments), regroup(d_out)))
    full_shape = tokens.shape
    acts = jnp.stack([middle.reshape(full_shape), final.reshape(full_shape)]).astype(jnp.bfloat16)
    input_grad = jnp.stack([d_inputs.reshape(full_shape), d_middle.reshape(full_shape)]).astype(jnp.bfloat16)
    grads = [jnp.stack([summed[0][which], summed[1][which]]) for which in range(6)]
    return (acts, input_grad, grads[0], grads[1], grads[2], grads[3], grads[4], grads[5])
```

```python
import functools

import jax
import jax.numpy as jnp
import numpy as np
from jax import lax
from jax.experimental import pallas as pl
from jax.experimental.pallas import tpu as pltpu
from jax.sharding import PartitionSpec as P

D = 960
HEADS = 15
KV_HEADS = 5
HEAD = 64
FF = 2560
SEQ = 128
EPS = 1e-05
BASE = 100000.0

DP = 1024
HALF = DP // 2
QKV = 1600
QKVP = 1664
QK = 1280
ROWS = 30
BF = jnp.bfloat16
F32 = jnp.float32
MESH = pl.DeviceIdType.MESH

CHUNKS = ((0, 0, QKVP), (1, 0, DP), (2, 0, FF), (2, FF, FF), (3, 0, FF))
WIDTHS = (QKVP, DP, 2 * FF, FF)
BACK_ORDER = (4, 2, 3, 1, 0)
N_AG = 18
N_RS = 12


def permutation():
    table = np.zeros((D, DP), np.float32)
    for d in range(D):
        f, r = divmod(d, ROWS)
        y, z, x = f // 8, (f // 2) % 4, f % 2
        h, rr = divmod(r, 16)
        at = (z * 2 + x) * 4 + y if h == 0 else (y * 2 + x) * 4 + z
        table[d, h * HALF + at * 16 + rr] = 1.0
    return table


def lane_frequencies():
    i = np.arange(128) % 32
    return np.power(np.float32(BASE), -(i.astype(np.float32)) * np.float32(2.0 / HEAD))[None, :].astype(np.float32)


def nn(a, b):
    return lax.dot_general(a, b, (((1,), (0,)), ((), ())), preferred_element_type=F32)


def nt(a, b):
    return lax.dot_general(a, b, (((1,), (1,)), ((), ())), preferred_element_type=F32)


def tn(a, b):
    return lax.dot_general(a, b, (((0,), (0,)), ((), ())), preferred_element_type=F32)


def over(total, tile, body):
    whole = total // tile

    @pl.loop(0, whole)
    def _(i):
        body(pl.ds(pl.multiple_of(i * tile, tile), tile))

    if total % tile:
        body(pl.ds(whole * tile, total % tile))


def kernel(
    tok, seg, ga, wq_in, wo_in, gf, wg_in, wd_in, dout, perm, freq,
    acts, igrad, gga, gq, go, ggf, gg, gd,
    wq, wo, wg, wd, *rest,
):
    n = len(CHUNKS)
    (pq, po, pg, pd), rest = rest[:4], rest[4:]
    rb, ra, rx, r3, fin = (rest[k * n:(k + 1) * n] for k in range(5))
    rest = rest[5 * n:]
    (
        raw, draw, xin, din, act, ig, a960, i960,
        qkv, qk, vv, pf, o, h, xn1, xn2, gate, up, mm,
        dgu, dh, da, do, dqkf, dqkv, lt, cosr, sinr, gains,
        ag_s, ag_r, rs_s, rs_r, mi_s, mi_r,
    ) = rest
    weights = (wq, wo, wg, wd)

    sec = lax.axis_index("section")
    f = lax.axis_index("fsdp")
    c = lax.axis_index("ctx")
    y = f // 8
    z = lax.rem(f // 2, 4)
    x = lax.rem(f, 2)
    a = y + c * (z - y)
    cc = z + c * (y - z)

    def at(a_, x_, cc_):
        yy = a_ + c * (cc_ - a_)
        zz = cc_ + c * (a_ - cc_)
        return (sec, (yy * 4 + zz) * 2 + x_, c)

    def mod4(v):
        return lax.rem(v + 4, 4)

    def row(cc_, x_, a_, half=None):
        half = c if half is None else half
        return pl.multiple_of(half * HALF + ((cc_ * 2 + x_) * 4 + a_) * 16, 16)

    sibling = (sec, f, 1 - c)
    partner = (1 - sec, f, c)
    other_x = 1 - x

    def remote(src, dst, ssem, rsem, dev):
        return pltpu.make_async_remote_copy(
            src_ref=src, dst_ref=dst, send_sem=ssem, recv_sem=rsem, device_id=dev, device_id_type=MESH
        )

    barrier = pltpu.get_barrier_semaphore()
    friends = [at(mod4(a + 1), x, cc), at(mod4(a + 2), x, cc), at(mod4(a + 3), x, cc), at(a, other_x, cc),
               at(a, x, mod4(cc + 1)), at(a, x, mod4(cc + 3)), sibling, partner]
    for dev in friends:
        pl.semaphore_signal(barrier, inc=1, device_id=dev, device_id_type=MESH)
    pl.semaphore_wait(barrier, len(friends))

    pending = []

    def send(src, dst, sems, k, dev):
        copy = remote(src, dst, sems[0].at[k], sems[1].at[k], dev)
        copy.start()
        pending.append(copy)

    def arrived(dst, sems, k):
        remote(dst, dst, sems[0].at[k], sems[1].at[k], sibling).wait_recv()

    def drain():
        for copy in pending:
            copy.wait_send()
        pending.clear()

    ag = (ag_s, ag_r)
    rs = (rs_s, rs_r)
    mi = (mi_s, mi_r)

    own_half = pl.ds(pl.multiple_of(64 * c, 64), 64)
    sib_half = pl.ds(pl.multiple_of(64 * (1 - c), 64), 64)
    send(tok.at[1 - c], raw.at[own_half], mi, 0, sibling)
    send(dout.at[1 - c], draw.at[own_half], mi, 1, sibling)
    raw[own_half, :] = tok[c]
    draw[own_half, :] = dout[c]

    gains[...] = jnp.zeros_like(gains)
    gains[0:1, 0:ROWS] = ga[...].astype(F32)
    gains[1:2, 0:ROWS] = gf[...].astype(F32)
    gain_cols = gains[0:8, 0:128].T
    for pack, source, cols in ((pq, wq_in, QKV), (po, wo_in, D), (pg, wg_in, 2 * FF), (pd, wd_in, FF)):
        pack[...] = jnp.zeros_like(pack)
        pack[0:ROWS, 0:cols] = source[...]
    pq[:, QKV:QKV + 2] = gain_cols[0:32, 0:2].astype(BF)
    own16 = pl.ds(pl.multiple_of(16 * c, 16), 16)
    for pack, w in ((pq, wq), (po, wo), (pg, wg), (pd, wd)):
        w[pl.ds(row(cc, x, a), 16), :] = pack[own16, :]

    def ag_piece(m, start, rows):
        w, first, cols = CHUNKS[m]
        return weights[w].at[pl.ds(start, rows), pl.ds(first, cols)]

    def ag_send(m, start, rows, k, dev):
        piece = ag_piece(m, start, rows)
        send(piece, piece, ag, m * N_AG + k, dev)

    def ag_arrived(m, start, rows, k):
        arrived(ag_piece(m, start, rows), ag, m * N_AG + k)

    last_up, last_down = at(a, x, mod4(cc + 1)), at(a, x, mod4(cc + 3))

    def ag0(m):
        for k, step in enumerate((1, 3, 2)):
            ag_send(m, row(cc, x, a), 16, k, at(mod4(a + step), x, cc))

    def ag1(m):
        for k, step in enumerate((1, 3, 2)):
            ag_arrived(m, row(cc, x, mod4(a - step)), 16, k)
        mine = row(cc, x, 0)
        ag_send(m, mine, 64, 3, at(a, other_x, cc))
        ag_send(m, mine, 64, 4, last_up)
        ag_send(m, mine, 64, 5, last_down)
        ag_send(m, mine, 64, 10, sibling)

    def ag2(m):
        theirs = row(cc, other_x, 0)
        ag_arrived(m, theirs, 64, 3)
        ag_send(m, theirs, 64, 6, last_up)
        ag_send(m, theirs, 64, 7, last_down)
        ag_send(m, theirs, 64, 11, sibling)
        below, above = row(mod4(cc - 1), x, 0), row(mod4(cc + 1), x, 0)
        ag_arrived(m, below, 64, 4)
        ag_send(m, below, 64, 8, last_up)
        ag_send(m, below, 64, 12, sibling)
        ag_arrived(m, above, 64, 5)
        ag_send(m, above, 64, 13, sibling)

    def ag3(m):
        below, above = row(mod4(cc - 1), other_x, 0), row(mod4(cc + 1), other_x, 0)
        ag_arrived(m, above, 64, 7)
        ag_send(m, above, 64, 9, last_down)
        ag_send(m, above, 64, 15, sibling)
        ag_arrived(m, below, 64, 6)
        ag_send(m, below, 64, 14, sibling)

    def ag4(m):
        far = row(mod4(cc + 2), x, 0)
        ag_arrived(m, far, 64, 8)
        ag_send(m, far, 64, 16, sibling)
        far = row(mod4(cc + 2), other_x, 0)
        ag_arrived(m, far, 64, 9)
        ag_send(m, far, 64, 17, sibling)

    def ag5(m):
        for k, (step, x_) in enumerate(((0, x), (0, other_x), (3, x), (1, x), (3, other_x), (1, other_x), (2, x), (2, other_x))):
            ag_arrived(m, row(mod4(a + step), x_, 0, 1 - c), 64, 10 + k)

    for m in range(n):
        ag0(m)
    stages = (ag1, ag2, ag3, ag4, ag5)
    for t in range(n + len(stages) - 1):
        for k in reversed(range(len(stages))):
            if 0 <= t - k < n:
                stages[k](t - k)

    places = lax.broadcasted_iota(jnp.int32, (SEQ, SEQ), 0)
    lanes = lax.broadcasted_iota(jnp.int32, (SEQ, SEQ), 1)
    key_seg = jnp.broadcast_to(seg[pl.ds(c, 1), :].astype(F32), (SEQ, SEQ))
    query_seg = key_seg.T
    allowed = (key_seg == query_seg) & (lanes <= places)
    earlier = jnp.sum(jnp.where(key_seg < query_seg, 1.0, 0.0), axis=1, keepdims=True)
    pos = places.astype(F32) - earlier
    angle = pos * freq[...]
    first_half = lax.rem(lanes, HEAD) < HEAD // 2
    cosr[...] = jnp.cos(angle)
    sinr[...] = jnp.where(first_half, -jnp.sin(angle), jnp.sin(angle))

    def swap(u):
        return jnp.where(first_half, pltpu.roll(u, 96, 1), pltpu.roll(u, 32, 1))

    arrived(raw.at[sib_half], mi, 0)
    arrived(draw.at[sib_half], mi, 1)
    drain()

    @pl.when(sec == 0)
    def _():
        xin[...] = nn(raw[...], perm[...]).astype(BF)

    @pl.when(sec == 1)
    def _():
        din[...] = nn(draw[...], perm[...]).astype(BF)
        arrived(xin, mi, 2)

    gain_rows = wq[:, 1536:1664].astype(F32).T[64:72, :]
    gain_one = gain_rows[0:1, :]
    gain_two = gain_rows[1:2, :]

    def norm(v):
        inverse = lax.rsqrt(jnp.sum(v * v, axis=1, keepdims=True) * (1.0 / D) + EPS)
        return v * inverse, inverse

    def norm_back(d, normal, inverse):
        return inverse * (d - normal * (jnp.sum(normal * d, axis=1, keepdims=True) * (1.0 / D)))

    xv = xin[...].astype(F32)
    xhat, _ = norm(xv)
    xn1[...] = (xhat * gain_one).astype(BF)

    def body_qkv(cols):
        qkv[:, cols] = nn(xn1[...], wq[:, cols])

    over(QKVP, 512, body_qkv)
    for t in range(QK // 128):
        cols = pl.ds(128 * t, 128)
        u = qkv[:, cols]
        qk[:, cols] = (u * cosr[...] + swap(u) * sinr[...]).astype(BF)
    vv[...] = qkv[:, QK:QKVP].astype(BF)
    o[:, HEADS * HEAD:] = jnp.zeros((SEQ, DP - HEADS * HEAD), BF)
    for g in range(KV_HEADS):
        k_g = qk[:, D + HEAD * g:D + HEAD * (g + 1)]
        v_g = vv[:, HEAD * g:HEAD * (g + 1)]
        for j in range(HEADS // KV_HEADS):
            hd = g * 3 + j
            s = nt(qk[:, HEAD * hd:HEAD * (hd + 1)], k_g) * (HEAD ** -0.5)
            s = jnp.where(allowed, s, -1e30)
            e = jnp.exp(s - jnp.max(s, axis=1, keepdims=True))
            p = e / jnp.sum(e, axis=1, keepdims=True)
            pf[hd] = p
            o[:, HEAD * hd:HEAD * (hd + 1)] = nn(p.astype(BF), v_g).astype(BF)

    def body_out(rows):
        h[:, rows] = xin[:, rows].astype(F32) + nt(o[...], wo[rows, :])

    over(DP, 256, body_out)
    xhat, _ = norm(h[...])
    xn2[...] = (xhat * gain_two).astype(BF)

    def body_gu(cols):
        first = cols.start
        g_ = nn(xn2[...], wg[:, pl.ds(first, 512)])
        u_ = nn(xn2[...], wg[:, pl.ds(pl.multiple_of(first + FF, 512), 512)])
        gate[:, cols] = g_
        up[:, cols] = u_
        mm[:, cols] = (g_ * jax.nn.sigmoid(g_) * u_).astype(BF)

    over(FF, 512, body_gu)

    def body_down(rows):
        act[:, rows] = (h[:, rows] + nt(mm[...], wd[rows, :])).astype(BF)

    over(DP, 256, body_down)

    @pl.when(sec == 0)
    def _():
        remote(act, xin, mi_s.at[2], mi_r.at[2], partner).start()

    a960[...] = nt(act[...], perm[...]).astype(BF)
    acts[c] = a960[own_half, :]
    send(a960.at[sib_half], acts.at[c], mi, 4, sibling)

    @pl.when(sec == 0)
    def _():
        remote(act, xin, mi_s.at[2], mi_r.at[2], partner).wait_send()
        arrived(din, mi, 3)

    def body_dm(cols):
        dm = nn(din[...], wd[:, cols])
        g_ = gate[:, cols]
        u_ = up[:, cols]
        sg = jax.nn.sigmoid(g_)
        dgu[:, cols] = (dm * u_ * sg * (1.0 + g_ * (1.0 - sg))).astype(BF)
        dgu[:, pl.ds(pl.multiple_of(cols.start + FF, 512), 512)] = (dm * g_ * sg).astype(BF)

    over(FF, 512, body_dm)

    def body_dxn2(rows):
        dh[:, rows] = nt(dgu[...], wg[rows, :])

    over(DP, 256, body_dxn2)
    xhat, inv = norm(h[...])
    dhv = din[...].astype(F32) + norm_back(dh[...] * gain_two, xhat, inv)
    dh[...] = dhv
    da[...] = dhv.astype(BF)

    def body_do(cols):
        do[:, cols] = nn(da[...], wo[:, cols]).astype(BF)

    over(DP, 512, body_do)
    scale = HEAD ** -0.5
    dqkv[:, QKV:] = jnp.zeros((SEQ, QKVP - QKV), BF)
    for g in range(KV_HEADS):
        k_g = qk[:, D + HEAD * g:D + HEAD * (g + 1)]
        v_g = vv[:, HEAD * g:HEAD * (g + 1)]
        dk, dv = None, None
        for j in range(HEADS // KV_HEADS):
            hd = g * 3 + j
            hc = slice(HEAD * hd, HEAD * (hd + 1))
            p = pf[hd]
            do_h = do[:, hc]
            dp = nt(do_h, v_g)
            ds = (p * (dp - jnp.sum(dp * p, axis=1, keepdims=True))).astype(BF)
            dqkf[:, hc] = nn(ds, k_g) * scale
            dk_h = tn(ds, qk[:, hc])
            dv_h = tn(p.astype(BF), do_h)
            dk = dk_h if dk is None else dk + dk_h
            dv = dv_h if dv is None else dv + dv_h
        dqkf[:, D + HEAD * g:D + HEAD * (g + 1)] = dk * scale
        dqkv[:, QK + HEAD * g:QK + HEAD * (g + 1)] = dv.astype(BF)
    for t in range(QK // 128):
        cols = pl.ds(128 * t, 128)
        u = dqkf[:, cols]
        dqkv[:, cols] = (u * cosr[...] - swap(u) * sinr[...]).astype(BF)

    def body_dxn1(rows):
        h[:, rows] = nt(dqkv[...], wq[rows, :])

    over(DP, 256, body_dxn1)
    xhat, inv = norm(xin[...].astype(F32))
    ig[...] = (dh[...] + norm_back(h[...] * gain_one, xhat, inv)).astype(BF)

    @pl.when(sec == 1)
    def _():
        remote(ig, din, mi_s.at[3], mi_r.at[3], partner).start()

    def wgrad(left, right, w, first, cols):
        lt[...] = left[...].T

        def body(tile):
            width = tile.size
            mine = pl.ds(pl.multiple_of(tile.start + first, 128), width)
            for r in range(4):
                rows = pl.ds(256 * r, 256)
                w[rows, mine] = nn(lt[rows, :], right[:, mine]).astype(BF)

        over(cols, 512, body)

    pairs = ((xn1, dqkv), (da, o), (xn2, dgu), (din, mm))

    def rs_piece(m, start, rows):
        w, first, cols = CHUNKS[m]
        return weights[w].at[pl.ds(start, rows), pl.ds(first, cols)]

    def add_in(m, start, rows, source, source_row):
        w, first, cols = CHUNKS[m]
        ref = weights[w]

        def body(tile):
            mine = pl.ds(pl.multiple_of(tile.start + first, 128), tile.size)
            ref[pl.ds(start, rows), mine] = ref[pl.ds(start, rows), mine] + source[pl.ds(source_row, rows), tile]

        over(cols, 512, body)

    def rs_send(m, start, rows, dst, k, dev):
        send(rs_piece(m, start, rows), dst, rs, m * N_RS + k, dev)

    def rs_arrived(m, dst, k):
        arrived(dst, rs, m * N_RS + k)

    def part(m, k):
        return ra[m].at[pl.ds(64 * k, 64)]

    nxt, prv, far = mod4(cc + 1), mod4(cc - 1), mod4(cc + 2)

    def rs0(m):
        w, first, cols = CHUNKS[m]
        wgrad(*pairs[w], weights[w], first, cols)
        rs_send(m, pl.multiple_of((1 - c) * HALF, HALF), HALF, rb[m], 0, sibling)

    def rs1(m):
        rs_arrived(m, rb[m], 0)
        add_in(m, pl.multiple_of(c * HALF, HALF), HALF, rb[m], 0)
        rs_send(m, row(far, 0, 0), 64, part(m, 0), 1, last_up)
        rs_send(m, row(far, 1, 0), 64, part(m, 1), 2, last_down)
        rs_send(m, row(nxt, 1, 0), 64, part(m, 2), 3, last_up)
        rs_send(m, row(prv, 0, 0), 64, part(m, 3), 4, last_down)

    def rs2(m):
        rs_arrived(m, part(m, 0), 1)
        add_in(m, row(nxt, 0, 0), 64, ra[m], 0)
        rs_send(m, row(nxt, 0, 0), 64, part(m, 4), 5, last_up)
        rs_arrived(m, part(m, 1), 2)
        add_in(m, row(prv, 1, 0), 64, ra[m], 64)
        rs_send(m, row(prv, 1, 0), 64, part(m, 5), 6, last_down)

    def rs3(m):
        for k, x_, sem in ((2, 1, 3), (3, 0, 4), (4, 0, 5), (5, 1, 6)):
            rs_arrived(m, part(m, k), sem)
            add_in(m, row(cc, x_, 0), 64, ra[m], 64 * k)
        rs_send(m, row(cc, other_x, 0), 64, rx[m], 7, at(a, other_x, cc))

    def rs4(m):
        rs_arrived(m, rx[m], 7)
        add_in(m, row(cc, x, 0), 64, rx[m], 0)
        for k, step in enumerate((1, 3, 2)):
            to = mod4(a + step)
            rs_send(m, row(cc, x, to), 16, r3[m].at[pl.ds(16 * k, 16)], 8 + k, at(to, x, cc))

    def rs5(m):
        w, first, cols = CHUNKS[m]
        for k in range(3):
            rs_arrived(m, r3[m].at[pl.ds(16 * k, 16)], 8 + k)
        total = weights[w][pl.ds(row(cc, x, a), 16), pl.ds(first, cols)].astype(F32)
        for k in range(3):
            total = total + r3[m][pl.ds(16 * k, 16), :].astype(F32)
        fin[m][own16, :] = total
        mine = fin[m].at[own16]
        send(mine, mine, rs, m * N_RS + 11, sibling)

    def rs6(m):
        rs_arrived(m, fin[m].at[pl.ds(pl.multiple_of(16 * (1 - c), 16), 16)], 11)

    stages = (rs0, rs1, rs2, rs3, rs4, rs5, rs6)
    for t in range(n + len(stages) - 1):
        for k in reversed(range(len(stages))):
            if 0 <= t - k < n:
                stages[k](BACK_ORDER[t - k])

    gq[...] = fin[0][0:ROWS, 0:QKV]
    go[...] = fin[1][0:ROWS, 0:D]
    gg[:, 0:FF] = fin[2][0:ROWS, :]
    gg[:, FF:] = fin[3][0:ROWS, :]
    gd[...] = fin[4][0:ROWS, :]
    sum_one = jnp.sum(fin[0][:, 0:QKV] * pq[:, 0:QKV].astype(F32), axis=1, keepdims=True)
    sum_two = jnp.sum(
        fin[2][...] * pg[:, 0:FF].astype(F32) + fin[3][...] * pg[:, FF:].astype(F32), axis=1, keepdims=True
    )
    gga[...] = jnp.broadcast_to(sum_one, (32, 128)).T[0:1, 0:ROWS] / ga[...].astype(F32)
    ggf[...] = jnp.broadcast_to(sum_two, (32, 128)).T[0:1, 0:ROWS] / gf[...].astype(F32)

    i960[...] = nt(ig[...], perm[...]).astype(BF)
    igrad[c] = i960[own_half, :]
    send(i960.at[sib_half], igrad.at[c], mi, 5, sibling)
    arrived(acts.at[1 - c], mi, 4)
    arrived(igrad.at[1 - c], mi, 5)

    @pl.when(sec == 1)
    def _():
        remote(ig, din, mi_s.at[3], mi_r.at[3], partner).wait_send()

    drain()


def per_device(tokens, segments, gain_attn, w_qkv, w_out, gain_ffn, w_gu, w_down, d_out):
    n = len(CHUNKS)
    vmem = pl.BlockSpec(memory_space=pltpu.VMEM)
    per_chunk = lambda rows, kind: [pltpu.VMEM((rows, cols), kind) for _, _, cols in CHUNKS]
    scratch = (
        [pltpu.VMEM((DP, w), BF) for w in WIDTHS]
        + [pltpu.VMEM((32, w), BF) for w in WIDTHS]
        + per_chunk(HALF, BF) + per_chunk(384, BF) + per_chunk(64, BF) + per_chunk(48, BF) + per_chunk(32, F32)
        + [
            pltpu.VMEM((SEQ, D), BF), pltpu.VMEM((SEQ, D), BF),
            pltpu.VMEM((SEQ, DP), BF), pltpu.VMEM((SEQ, DP), BF),
            pltpu.VMEM((SEQ, DP), BF), pltpu.VMEM((SEQ, DP), BF),
            pltpu.VMEM((SEQ, D), BF), pltpu.VMEM((SEQ, D), BF),
            pltpu.VMEM((SEQ, QKVP), F32), pltpu.VMEM((SEQ, QK), BF), pltpu.VMEM((SEQ, QKVP - QK), BF),
            pltpu.VMEM((HEADS, SEQ, SEQ), F32), pltpu.VMEM((SEQ, DP), BF), pltpu.VMEM((SEQ, DP), F32),
            pltpu.VMEM((SEQ, DP), BF), pltpu.VMEM((SEQ, DP), BF),
            pltpu.VMEM((SEQ, FF), F32), pltpu.VMEM((SEQ, FF), F32), pltpu.VMEM((SEQ, FF), BF),
            pltpu.VMEM((SEQ, 2 * FF), BF), pltpu.VMEM((SEQ, DP), F32),
            pltpu.VMEM((SEQ, DP), BF), pltpu.VMEM((SEQ, DP), BF),
            pltpu.VMEM((SEQ, QK), F32), pltpu.VMEM((SEQ, QKVP), BF), pltpu.VMEM((DP, SEQ), BF),
            pltpu.VMEM((SEQ, SEQ), F32), pltpu.VMEM((SEQ, SEQ), F32), pltpu.VMEM((8, 128), F32),
        ]
        + [pltpu.SemaphoreType.DMA((n * N_AG,))] * 2
        + [pltpu.SemaphoreType.DMA((n * N_RS,))] * 2
        + [pltpu.SemaphoreType.DMA((6,))] * 2
    )
    shape = jax.ShapeDtypeStruct
    out = pl.pallas_call(
        kernel,
        out_shape=(
            shape(tokens.shape, BF), shape(tokens.shape, BF),
            shape((1, ROWS), F32), shape((ROWS, QKV), F32), shape((ROWS, D), F32),
            shape((1, ROWS), F32), shape((ROWS, 2 * FF), F32), shape((ROWS, FF), F32),
        ),
        in_specs=[vmem] * 11,
        out_specs=(vmem,) * 8,
        scratch_shapes=scratch,
        compiler_params=pltpu.CompilerParams(
            collective_id=0, has_side_effects=True, vmem_limit_bytes=63 * 1024 * 1024
        ),
    )(
        tokens, segments, gain_attn, w_qkv[0], w_out[0], gain_ffn, w_gu[0], w_down[0], d_out,
        jnp.asarray(permutation(), BF), jnp.asarray(lane_frequencies(), F32),
    )
    acts, igrad, gga, gq, go, ggf, gg, gd = out
    return acts[None], igrad[None], gga, gq[None], go[None], ggf, gg[None], gd[None]


def solution(mesh):
    in_specs = (
        P(None, ("fsdp", "ctx"), None),
        P(None, "fsdp"),
        P("section", "fsdp"),
        P("section", "fsdp", None),
        P("section", "fsdp", None),
        P("section", "fsdp"),
        P("section", "fsdp", None),
        P("section", "fsdp", None),
        P(None, ("fsdp", "ctx"), None),
    )
    out_specs = (
        P("section", None, ("fsdp", "ctx"), None),
        P("section", None, ("fsdp", "ctx"), None),
        P("section", "fsdp"),
        P("section", "fsdp", None),
        P("section", "fsdp", None),
        P("section", "fsdp"),
        P("section", "fsdp", None),
        P("section", "fsdp", None),
    )
    return jax.shard_map(
        per_device, mesh=mesh, in_specs=in_specs, out_specs=out_specs, check_vma=False
    )
```

```python
import functools

import jax
import jax.numpy as jnp
import numpy as np
from jax import lax
from jax.experimental import pallas as pl
from jax.experimental.pallas import tpu as pltpu
from jax.sharding import PartitionSpec as P

D = 960
HEADS = 15
KV_HEADS = 5
HEAD = 64
FF = 2560
SEQ = 128
EPS = 1e-05
BASE = 100000.0

DP = 1024
HALF = DP // 2
QKV = 1600
QKVP = 1664
QK = 1280
ROWS = 30
BF = jnp.bfloat16
F32 = jnp.float32
MESH = pl.DeviceIdType.MESH

PART = FF // 2
CHUNKS = (
    (0, 0, QKVP), (1, 0, DP), (2, 0, PART), (2, FF, PART), (2, PART, PART), (2, FF + PART, PART), (3, 0, PART), (3, PART, PART),
)
WIDTHS = (QKVP, DP, 2 * FF, FF)
BACK_ORDER = (6, 7, 2, 3, 4, 5, 1, 0)
N_AG = 18
N_RS = 12


def permutation():
    table = np.zeros((D, DP), np.float32)
    for d in range(D):
        f, r = divmod(d, ROWS)
        y, z, x = f // 8, (f // 2) % 4, f % 2
        h, rr = divmod(r, 16)
        at = (z * 2 + x) * 4 + y if h == 0 else (y * 2 + x) * 4 + z
        table[d, h * HALF + at * 16 + rr] = 1.0
    return table


def lane_frequencies():
    i = np.arange(128) % 32
    return np.power(np.float32(BASE), -(i.astype(np.float32)) * np.float32(2.0 / HEAD))[None, :].astype(np.float32)


def nn(a, b):
    return lax.dot_general(a, b, (((1,), (0,)), ((), ())), preferred_element_type=F32)


def nt(a, b):
    return lax.dot_general(a, b, (((1,), (1,)), ((), ())), preferred_element_type=F32)


def tn(a, b):
    return lax.dot_general(a, b, (((0,), (0,)), ((), ())), preferred_element_type=F32)


def over(total, tile, body):
    whole = total // tile

    @pl.loop(0, whole)
    def _(i):
        body(pl.ds(pl.multiple_of(i * tile, tile), tile))

    if total % tile:
        body(pl.ds(whole * tile, total % tile))


def kernel(
    tok, seg, ga, wq_in, wo_in, gf, wg_in, wd_in, dout, perm_in, freq,
    acts, igrad, gga, ggf, *rest,
):
    n = len(CHUNKS)
    fin, rest = rest[:n], rest[n:]
    (wq, wo, wg, wd), rest = rest[:4], rest[4:]
    shards, rest = rest[:4], rest[4:]
    (pq, po, pg, pd), rest = rest[:4], rest[4:]
    rb, ra, rx, r3 = (rest[k * n:(k + 1) * n] for k in range(4))
    rest = rest[4 * n:]
    lts, rest = rest[:4], rest[4:]
    (
        perm, raw, draw, xin, din, act, ig, a960, i960,
        qkv, qk, vv, pf, o, h, xn1, xn2, gate, up, mm,
        dgu, dh, da, do, dps, dsb, dqkf, dqkv, cosr, sinr, gains,
        in_s, ag_s, ag_r, rs_s, rs_r, mi_s, mi_r,
    ) = rest
    weights = (wq, wo, wg, wd)

    sec = lax.axis_index("section")
    f = lax.axis_index("fsdp")
    c = lax.axis_index("ctx")
    y = f // 8
    z = lax.rem(f // 2, 4)
    x = lax.rem(f, 2)
    a = y + c * (z - y)
    cc = z + c * (y - z)
    other_x = 1 - x

    def at(a_, x_, cc_):
        yy = a_ + c * (cc_ - a_)
        zz = cc_ + c * (a_ - cc_)
        return (sec, (yy * 4 + zz) * 2 + x_, c)

    def mod4(v):
        return lax.rem(v + 4, 4)

    def row(cc_, x_, a_, half=None):
        half = c if half is None else half
        return pl.multiple_of(half * HALF + ((cc_ * 2 + x_) * 4 + a_) * 16, 16)

    own_half = pl.ds(pl.multiple_of(64 * c, 64), 64)
    sib_half = pl.ds(pl.multiple_of(64 * (1 - c), 64), 64)
    own16 = pl.ds(pl.multiple_of(16 * c, 16), 16)
    fetch = [
        pltpu.make_async_copy(src, dst, in_s.at[k])
        for k, (src, dst) in enumerate((
            (wq_in, shards[0]), (wo_in, shards[1]), (wg_in, shards[2]), (wd_in, shards[3]),
            (tok.at[c], raw.at[own_half]), (dout.at[c], draw.at[own_half]), (perm_in, perm),
        ))
    ]
    for copy in fetch:
        copy.start()

    sibling = (sec, f, 1 - c)
    partner = (1 - sec, f, c)
    last_up, last_down = at(a, x, mod4(cc + 1)), at(a, x, mod4(cc + 3))
    over_x = at(a, other_x, cc)
    first_to = [at(mod4(a + step), x, cc) for step in (1, 3, 2)]

    barrier = pltpu.get_barrier_semaphore()
    friends = first_to + [over_x, last_up, last_down, sibling, partner]
    for dev in friends:
        pl.semaphore_signal(barrier, inc=1, device_id=dev, device_id_type=MESH)

    gains[...] = jnp.zeros_like(gains)
    gains[0:1, 0:ROWS] = ga[...].astype(F32)
    gains[1:2, 0:ROWS] = gf[...].astype(F32)
    gain_cols = gains[0:8, 0:128].T
    pl.semaphore_wait(barrier, len(friends))

    def remote(src, dst, ssem, rsem, dev):
        return pltpu.make_async_remote_copy(
            src_ref=src, dst_ref=dst, send_sem=ssem, recv_sem=rsem, device_id=dev, device_id_type=MESH
        )

    own_cols = [pl.ds(256 * k, 256) for k in range(4)]
    single = (
        [(tok.at[1 - c], raw.at[own_half], sibling), (dout.at[1 - c], draw.at[own_half], sibling)]
        + [(act.at[:, cols], xin.at[:, cols], partner) for cols in own_cols]
        + [(ig, din, partner), (a960.at[sib_half], acts.at[c], sibling), (i960.at[sib_half], igrad.at[c], sibling)]
    )

    def one(k):
        src, dst, dev = single[k]
        return remote(src, dst, mi_s.at[k], mi_r.at[k], dev)

    steps4 = range(4)
    xs = (x, other_x)
    mine = {(d, s): row(mod4(cc + d), xs[s], 0) for d in steps4 for s in range(2)}
    theirs = {(d, s): row(mod4(a + d), xs[s], 0, 1 - c) for d in steps4 for s in range(2)}
    slab = [row(cc, x, mod4(a + d)) for d in steps4]
    ag_table = [
        (slab[0], slab[3], 16, first_to[0]),
        (slab[0], slab[1], 16, first_to[1]),
        (slab[0], slab[2], 16, first_to[2]),
        (mine[0, 0], mine[0, 1], 64, over_x),
        (mine[0, 0], mine[3, 0], 64, last_up),
        (mine[0, 0], mine[1, 0], 64, last_down),
        (mine[0, 1], mine[3, 1], 64, last_up),
        (mine[0, 1], mine[1, 1], 64, last_down),
        (mine[3, 0], mine[2, 0], 64, last_up),
        (mine[1, 1], mine[2, 1], 64, last_down),
    ] + [
        (mine[key], theirs[key], 64, sibling)
        for key in ((0, 0), (0, 1), (3, 0), (1, 0), (3, 1), (1, 1), (2, 0), (2, 1))
    ]

    def ag_copy(m, k, arriving=False):
        w, first, cols = CHUNKS[m]
        source, landing, rows, dev = ag_table[k]
        piece = weights[w].at[pl.ds(landing if arriving else source, rows), pl.ds(first, cols)]
        return remote(piece, piece, ag_s.at[m * N_AG + k], ag_r.at[m * N_AG + k], dev)

    def ag_send(m, *ks):
        for k in ks:
            ag_copy(m, k).start()

    def ag_wait(m, *ks):
        for k in ks:
            ag_copy(m, k, True).wait_recv()

    def ag1(m):
        ag_wait(m, 0, 1, 2)
        ag_send(m, 4, 5, 3, 10)

    def ag2(m):
        ag_wait(m, 3)
        ag_send(m, 6, 7, 11)
        ag_wait(m, 4)
        ag_send(m, 8, 12)
        ag_wait(m, 5)
        ag_send(m, 13)

    def ag3(m):
        ag_wait(m, 7)
        ag_send(m, 9, 15)
        ag_wait(m, 6)
        ag_send(m, 14)

    def ag4(m):
        ag_wait(m, 8)
        ag_send(m, 16)
        ag_wait(m, 9)
        ag_send(m, 17)

    def ag5(m):
        ag_wait(m, *range(10, 18))

    def ag_step(t):
        for stage, late in ((ag1, 0), (ag5, 4), (ag4, 3), (ag3, 2), (ag2, 1)):
            if 0 <= t - late < n:
                stage(t - late)

    def ag_drain():
        for m in range(n):
            for k in range(N_AG):
                ag_copy(m, k).wait_send()

    one(0).start()
    for w, (pack, cols) in enumerate(((pq, QKV), (po, D), (pg, 2 * FF), (pd, FF))):
        if cols < pack.shape[1]:
            pack[:, cols:] = jnp.zeros((32, pack.shape[1] - cols), BF)
        pack[16:32, :] = jnp.zeros((16, pack.shape[1]), BF)
        fetch[w].wait()
        pack[0:ROWS, 0:cols] = shards[w][...]
        if w == 0:
            pack[:, QKV:QKV + 2] = gain_cols[0:32, 0:2].astype(BF)
        weights[w][pl.ds(slab[0], 16), :] = pack[own16, :]
        for m in range(n):
            if CHUNKS[m][0] == w:
                ag_send(m, 0, 1, 2)
    one(1).start()

    places = lax.broadcasted_iota(jnp.int32, (SEQ, SEQ), 0)
    lanes = lax.broadcasted_iota(jnp.int32, (SEQ, SEQ), 1)
    key_seg = jnp.broadcast_to(seg[pl.ds(c, 1), :].astype(F32), (SEQ, SEQ))
    query_seg = key_seg.T
    allowed = (key_seg == query_seg) & (lanes <= places)
    earlier = jnp.sum(jnp.where(key_seg < query_seg, 1.0, 0.0), axis=1, keepdims=True)
    pos = places.astype(F32) - earlier
    angle = pos * freq[...]
    first_half = lax.rem(lanes, HEAD) < HEAD // 2
    cosr[...] = jnp.cos(angle)
    sinr[...] = jnp.where(first_half, -jnp.sin(angle), jnp.sin(angle))

    def swap(u):
        return jnp.where(first_half, pltpu.roll(u, 96, 1), pltpu.roll(u, 32, 1))

    ag_step(0)
    for copy in fetch[4:]:
        copy.wait()
    for k in range(2):
        src, _, dev = single[k]
        remote(src, (raw, draw)[k].at[sib_half], mi_s.at[k], mi_r.at[k], dev).wait_recv()

    @pl.when(sec == 0)
    def _():
        xin[...] = nn(raw[...], perm[...]).astype(BF)

    @pl.when(sec == 1)
    def _():
        din[...] = nn(draw[...], perm[...]).astype(BF)

    def ag_first(*ts):
        @pl.when(sec == 0)
        def _():
            for t in ts:
                ag_step(t)

    @pl.when(sec == 1)
    def _():
        for t in range(1, n + 4):
            ag_step(t)
        ag_drain()
        for k in range(2, 6):
            one(k).wait_recv()

    ag_first(1, 2, 3, 4)

    def norm(v):
        inverse = lax.rsqrt(jnp.sum(v * v, axis=1, keepdims=True) * (1.0 / D) + EPS)
        return v * inverse, inverse

    def norm_back(d, normal, inverse):
        return inverse * (d - normal * (jnp.sum(normal * d, axis=1, keepdims=True) * (1.0 / D)))

    gains[...] = wq[:, 1536:1664].astype(F32).T[64:72, :]
    xhat, _ = norm(xin[...].astype(F32))
    xn1[...] = (xhat * gains[0:1, :]).astype(BF)
    qkv[...] = nn(xn1[...], wq[...])
    for t in range(QK // 128):
        cols = pl.ds(128 * t, 128)
        u = qkv[:, cols]
        qk[:, cols] = (u * cosr[...] + swap(u) * sinr[...]).astype(BF)
    vv[...] = qkv[:, QK:QKVP].astype(BF)
    ag_first(5)
    group = HEADS // KV_HEADS

    def head(hd):
        return slice(HEAD * hd, HEAD * (hd + 1))

    def key_of(hd):
        return qk[:, head(HEADS + hd // group)]

    def value_of(hd):
        return vv[:, head(hd // group)]

    scale = HEAD ** -0.5
    for hd in range(HEADS):
        pf[hd] = nt(qk[:, head(hd)], key_of(hd))
    for hd in range(HEADS):
        s = jnp.where(allowed, pf[hd] * scale, -1e30)
        e = jnp.exp(s - jnp.max(s, axis=1, keepdims=True))
        pf[hd] = e / jnp.sum(e, axis=1, keepdims=True)
    ag_first(6)
    o[:, HEADS * HEAD:] = jnp.zeros((SEQ, DP - HEADS * HEAD), BF)
    for hd in range(HEADS):
        o[:, head(hd)] = nn(pf[hd].astype(BF), value_of(hd)).astype(BF)
    h[...] = xin[...].astype(F32) + nt(o[...], wo[...])
    xhat, _ = norm(h[...])
    xn2[...] = (xhat * gains[1:2, :]).astype(BF)
    ag_first(7)

    def gated(j):
        cols = pl.ds(PART * j, PART)
        gate[:, cols] = nn(xn2[...], wg[:, cols])
        up[:, cols] = nn(xn2[...], wg[:, pl.ds(FF + PART * j, PART)])
        g_ = gate[:, cols]
        mm[:, cols] = (g_ * jax.nn.sigmoid(g_) * up[:, cols]).astype(BF)

    gated(0)
    ag_first(8, 9)
    gated(1)
    ag_first(10)
    dh[...] = h[...] + nt(mm[:, 0:PART], wd[:, 0:PART])
    ag_first(11)
    for k, cols in enumerate(own_cols):
        act[:, cols] = (dh[:, cols] + nt(mm[:, PART:], wd[cols, PART:])).astype(BF)

        @pl.when(sec == 0)
        def _():
            one(2 + k).start()

    @pl.when(sec == 0)
    def _():
        ag_drain()
        for k in range(2, 6):
            one(k).wait_send()
        one(6).wait_recv()

    pairs = ((xn1, dqkv), (da, o), (xn2, dgu), (din, mm))
    last_at = [mod4(cc + d) for d in steps4]
    block = {(d, x_): row(last_at[d], x_, 0) for d in steps4 for x_ in range(2)}
    lower = pl.multiple_of(c * HALF, HALF)
    upper = pl.multiple_of((1 - c) * HALF, HALF)
    rs_rows = (
        [(upper, HALF, sibling), (block[2, 0], 64, last_up), (block[2, 1], 64, last_down), (block[1, 1], 64, last_up),
         (block[3, 0], 64, last_down), (block[1, 0], 64, last_up), (block[3, 1], 64, last_down), (mine[0, 1], 64, over_x)]
        + [(slab[step], 16, first_to[k]) for k, step in enumerate((1, 3, 2))]
    )

    def rs_copy(m, k):
        w, first, cols = CHUNKS[m]
        sems = rs_s.at[m * N_RS + k], rs_r.at[m * N_RS + k]
        if k == 11:
            piece = fin[m].at[own16]
            return remote(piece, piece, *sems, sibling)
        start, rows, dev = rs_rows[k]
        if k == 0:
            dst = rb[m]
        elif k < 7:
            dst = ra[m].at[pl.ds(64 * (k - 1), 64)]
        elif k == 7:
            dst = rx[m]
        else:
            dst = r3[m].at[pl.ds(16 * (k - 8), 16)]
        return remote(weights[w].at[pl.ds(start, rows), pl.ds(first, cols)], dst, *sems, dev)

    def rs_send(m, *ks):
        for k in ks:
            rs_copy(m, k).start()

    def rs_wait(m, *ks):
        for k in ks:
            rs_copy(m, k).wait_recv()

    def add_in(m, start, rows, source, source_row):
        w, first, cols = CHUNKS[m]
        ref = weights[w]
        width = PART // 2 if cols == PART else 512

        def body(tile):
            there = pl.ds(pl.multiple_of(tile.start + first, 128), tile.size)
            ref[pl.ds(start, rows), there] = ref[pl.ds(start, rows), there] + source[pl.ds(source_row, rows), tile]

        over(cols, width, body)

    def rs0(m):
        w, first, cols = CHUNKS[m]
        left, right = pairs[w]
        if first == 0:
            lts[w][...] = left[...].T

        def body(tile):
            there = pl.ds(pl.multiple_of(tile.start + first, 128), tile.size)
            for r in range(4):
                rows = pl.ds(256 * r, 256)
                weights[w][rows, there] = nn(lts[w][rows, :], right[:, there]).astype(BF)

        over(cols, 256, body)
        rs_send(m, 0)

    def rs1(m):
        rs_wait(m, 0)
        add_in(m, lower, HALF, rb[m], 0)
        rs_send(m, 1, 2, 3, 4)

    def rs2(m):
        rs_wait(m, 1)
        add_in(m, block[1, 0], 64, ra[m], 0)
        rs_send(m, 5)
        rs_wait(m, 2)
        add_in(m, block[3, 1], 64, ra[m], 64)
        rs_send(m, 6)

    def rs3(m):
        for k, x_ in ((3, 1), (4, 0), (5, 0), (6, 1)):
            rs_wait(m, k)
            add_in(m, block[0, x_], 64, ra[m], 64 * (k - 1))
        rs_send(m, 7)

    def rs4(m):
        rs_wait(m, 7)
        add_in(m, mine[0, 0], 64, rx[m], 0)
        rs_send(m, 8, 9, 10)

    def rs5(m):
        w, first, cols = CHUNKS[m]
        rs_wait(m, 8, 9, 10)
        total = weights[w][pl.ds(slab[0], 16), pl.ds(first, cols)].astype(F32)
        for k in range(3):
            total = total + r3[m][pl.ds(16 * k, 16), :].astype(F32)
        fin[m][own16, :] = total
        rs_send(m, 11)

    def rs6(m):
        remote(fin[m].at[own16], fin[m].at[pl.ds(pl.multiple_of(16 * (1 - c), 16), 16)],
               rs_s.at[m * N_RS + 11], rs_r.at[m * N_RS + 11], sibling).wait_recv()
        for k in range(N_RS):
            rs_copy(m, k).wait_send()

    stages = (rs0, rs1, rs2, rs3, rs4, rs5, rs6)

    def reduce(*jobs):
        for job in jobs:
            stages[job // 10](BACK_ORDER[job % 10])

    def reduce_first(*jobs):
        @pl.when(sec == 0)
        def _():
            reduce(*jobs)

    for j in range(2):
        cols = pl.ds(PART * j, PART)
        dm = nn(din[...], wd[:, cols])
        g_ = gate[:, cols]
        sg = jax.nn.sigmoid(g_)
        dgu[:, cols] = (dm * up[:, cols] * sg * (1.0 + g_ * (1.0 - sg))).astype(BF)
        dgu[:, pl.ds(FF + PART * j, PART)] = (dm * g_ * sg).astype(BF)
    reduce_first(0, 1)
    dh[...] = nt(dgu[...], wg[...])
    reduce_first(10, 2, 11, 3)
    xhat, inv = norm(h[...])
    dhv = din[...].astype(F32) + norm_back(dh[...] * gains[1:2, :], xhat, inv)
    dh[...] = dhv
    da[...] = dhv.astype(BF)
    do[...] = nn(da[...], wo[...]).astype(BF)
    reduce_first(20, 4, 12, 5)
    for hd in range(HEADS):
        dps[hd] = nt(do[:, head(hd)], value_of(hd))
    for hd in range(HEADS):
        p, dp = pf[hd], dps[hd]
        dsb[hd] = (p * (dp - jnp.sum(dp * p, axis=1, keepdims=True))).astype(BF)
    reduce_first(21, 13, 30)
    dqkv[:, QKV:] = jnp.zeros((SEQ, QKVP - QKV), BF)
    for hd in range(HEADS):
        dqkf[:, head(hd)] = nn(dsb[hd], key_of(hd)) * scale
    for g in range(KV_HEADS):
        hds = range(group * g, group * (g + 1))
        dqkf[:, head(HEADS + g)] = sum(tn(dsb[hd], qk[:, head(hd)]) for hd in hds) * scale
        dv = sum(tn(pf[hd].astype(BF), do[:, head(hd)]) for hd in hds)
        dqkv[:, QK + HEAD * g:QK + HEAD * (g + 1)] = dv.astype(BF)
    reduce_first(14, 6, 22, 31, 40)
    for t in range(QK // 128):
        cols = pl.ds(128 * t, 128)
        u = dqkf[:, cols]
        dqkv[:, cols] = (u * cosr[...] - swap(u) * sinr[...]).astype(BF)
    h[...] = nt(dqkv[...], wq[...])
    reduce_first(15, 23, 32, 41, 50)
    xhat, inv = norm(xin[...].astype(F32))
    ig[...] = (dh[...] + norm_back(h[...] * gains[0:1, :], xhat, inv)).astype(BF)

    @pl.when(sec == 1)
    def _():
        one(6).start()
        reduce(0, 1, 10, 2, 11, 3, 20, 4, 12, 5, 21, 13, 30, 14, 6, 22, 31, 40, 15, 23, 32, 41, 50)

    reduce(7, 16, 24, 33, 42, 51, 60)
    reduce(17, 25, 34, 43, 52, 61)
    a960[...] = nt(act[...], perm[...]).astype(BF)
    acts[c] = a960[own_half, :]
    one(7).start()
    i960[...] = nt(ig[...], perm[...]).astype(BF)
    igrad[c] = i960[own_half, :]
    one(8).start()
    reduce(26, 35, 44, 53, 62)
    reduce(27, 36, 45, 54, 63, 37, 46, 55, 64)

    for k in (7, 8):
        src, dst, dev = single[k]
        remote(src, (acts, igrad)[k - 7].at[1 - c], mi_s.at[k], mi_r.at[k], dev).wait_recv()
        one(k).wait_send()

    @pl.when(sec == 1)
    def _():
        one(6).wait_send()

    one(0).wait_send()
    one(1).wait_send()
    reduce(47, 56, 65)
    sum_two = sum(
        jnp.sum(fin[k][...] * pg[:, first:first + PART].astype(F32), axis=1, keepdims=True)
        for k, first in ((2, 0), (3, FF), (4, PART), (5, FF + PART))
    )
    ggf[...] = jnp.broadcast_to(sum_two, (32, 128)).T[0:1, 0:ROWS] / gf[...].astype(F32)
    reduce(57, 66)
    reduce(67)
    sum_one = jnp.sum(fin[0][:, 0:QKV] * pq[:, 0:QKV].astype(F32), axis=1, keepdims=True)
    gga[...] = jnp.broadcast_to(sum_one, (32, 128)).T[0:1, 0:ROWS] / ga[...].astype(F32)


def lay_out(*refs):
    n = len(CHUNKS)
    passed, fin, rest = refs[:4], refs[4:4 + n], refs[4 + n:]
    acts, igrad, gga, ggf, gq, go, gg, gd = rest
    for source, target in zip(passed, (acts, igrad, gga, ggf)):
        target[...] = source[...]
    targets = (gq, go, gg, gd)
    for m, (w, first, cols) in enumerate(CHUNKS):
        cols = min(cols, (QKV, D, 2 * FF, FF)[w])
        targets[w][:, 0, first:first + cols] = fin[m][0:ROWS, 0:cols]


def per_device(tokens, segments, gain_attn, w_qkv, w_out, gain_ffn, w_gu, w_down, d_out):
    n = len(CHUNKS)
    vmem = pl.BlockSpec(memory_space=pltpu.VMEM)
    per_chunk = lambda rows, kind: [pltpu.VMEM((rows, cols), kind) for _, _, cols in CHUNKS]
    scratch = (
        [pltpu.VMEM((DP, w), BF) for w in WIDTHS]
        + [pltpu.VMEM((ROWS, w), BF) for w in (QKV, D, 2 * FF, FF)]
        + [pltpu.VMEM((32, w), BF) for w in WIDTHS]
        + per_chunk(HALF, BF) + per_chunk(384, BF) + per_chunk(64, BF) + per_chunk(48, BF)
        + [pltpu.VMEM((DP, SEQ), BF)] * 4
        + [
            pltpu.VMEM((D, DP), BF),
            pltpu.VMEM((SEQ, D), BF), pltpu.VMEM((SEQ, D), BF),
            pltpu.VMEM((SEQ, DP), BF), pltpu.VMEM((SEQ, DP), BF),
            pltpu.VMEM((SEQ, DP), BF), pltpu.VMEM((SEQ, DP), BF),
            pltpu.VMEM((SEQ, D), BF), pltpu.VMEM((SEQ, D), BF),
            pltpu.VMEM((SEQ, QKVP), F32), pltpu.VMEM((SEQ, QK), BF), pltpu.VMEM((SEQ, QKVP - QK), BF),
            pltpu.VMEM((HEADS, SEQ, SEQ), F32), pltpu.VMEM((SEQ, DP), BF), pltpu.VMEM((SEQ, DP), F32),
            pltpu.VMEM((SEQ, DP), BF), pltpu.VMEM((SEQ, DP), BF),
            pltpu.VMEM((SEQ, FF), F32), pltpu.VMEM((SEQ, FF), F32), pltpu.VMEM((SEQ, FF), BF),
            pltpu.VMEM((SEQ, 2 * FF), BF), pltpu.VMEM((SEQ, DP), F32),
            pltpu.VMEM((SEQ, DP), BF), pltpu.VMEM((SEQ, DP), BF),
            pltpu.VMEM((HEADS, SEQ, SEQ), F32), pltpu.VMEM((HEADS, SEQ, SEQ), BF),
            pltpu.VMEM((SEQ, QK), F32), pltpu.VMEM((SEQ, QKVP), BF),
            pltpu.VMEM((SEQ, SEQ), F32), pltpu.VMEM((SEQ, SEQ), F32), pltpu.VMEM((8, DP), F32),
        ]
        + [pltpu.SemaphoreType.DMA((7,))]
        + [pltpu.SemaphoreType.DMA((n * N_AG,))] * 2
        + [pltpu.SemaphoreType.DMA((n * N_RS,))] * 2
        + [pltpu.SemaphoreType.DMA((9,))] * 2
    )
    shape = jax.ShapeDtypeStruct
    hbm = pl.BlockSpec(memory_space=pl.ANY)
    passed = (shape(tokens.shape, BF), shape(tokens.shape, BF), shape((1, ROWS), F32), shape((1, ROWS), F32))
    out = pl.pallas_call(
        kernel,
        out_shape=passed + tuple(shape((32, cols), F32) for _, _, cols in CHUNKS),
        in_specs=[hbm, vmem, vmem, hbm, hbm, vmem, hbm, hbm, hbm, hbm, vmem],
        out_specs=(vmem,) * (4 + n),
        scratch_shapes=scratch,
        compiler_params=pltpu.CompilerParams(
            collective_id=0, has_side_effects=True, vmem_limit_bytes=63 * 1024 * 1024
        ),
    )(
        tokens, segments, gain_attn, w_qkv[0], w_out[0], gain_ffn, w_gu[0], w_down[0], d_out,
        jnp.asarray(permutation(), BF), jnp.asarray(lane_frequencies(), F32),
    )
    acts, igrad, gga, ggf, gq, go, gg, gd = pl.pallas_call(
        lay_out,
        out_shape=passed + tuple(shape((ROWS, 1, cols), F32) for cols in (QKV, D, 2 * FF, FF)),
        in_specs=[vmem] * (4 + n),
        out_specs=(vmem,) * 8,
    )(*out)
    gq, go, gg, gd = (jnp.swapaxes(g, 0, 1) for g in (gq, go, gg, gd))
    return acts[None], igrad[None], gga, gq, go, ggf, gg, gd


def solution(mesh):
    in_specs = (
        P(None, ("fsdp", "ctx"), None),
        P(None, "fsdp"),
        P("section", "fsdp"),
        P("section", "fsdp", None),
        P("section", "fsdp", None),
        P("section", "fsdp"),
        P("section", "fsdp", None),
        P("section", "fsdp", None),
        P(None, ("fsdp", "ctx"), None),
    )
    out_specs = (
        P("section", None, ("fsdp", "ctx"), None),
        P("section", None, ("fsdp", "ctx"), None),
        P("section", "fsdp"),
        P("section", "fsdp", None),
        P("section", "fsdp", None),
        P("section", "fsdp"),
        P("section", "fsdp", None),
        P("section", "fsdp", None),
    )
    return jax.shard_map(
        per_device, mesh=mesh, in_specs=in_specs, out_specs=out_specs, check_vma=False
    )
```

```python
import functools

import jax
import jax.numpy as jnp
import numpy as np
from jax import lax
from jax.experimental import pallas as pl
from jax.experimental.pallas import tpu as pltpu
from jax.sharding import PartitionSpec as P

D = 960
HEADS = 15
KV_HEADS = 5
HEAD = 64
FF = 2560
SEQ = 128
EPS = 1e-05
BASE = 100000.0

DP = 1024
HALF = DP // 2
QKV = 1600
QKVP = 1664
QK = 1280
ROWS = 30
BF = jnp.bfloat16
F32 = jnp.float32
MESH = pl.DeviceIdType.MESH

PART = FF // 2
PIECES = (
    (0, 0, QKVP, 1), (1, 0, DP, 0), (2, 0, PART, 1), (2, FF, PART, 0), (2, PART, PART, 1), (2, FF + PART, PART, 0),
    (3, 0, PART, 0), (3, PART, PART, 0),
)
SUMS = (
    (3, 0, 640), (2, 0, PART), (2, FF, PART), (2, PART, PART), (2, FF + PART, PART), (1, 0, DP), (0, 0, QKVP),
    (3, 640, 640), (3, PART, 640), (3, PART + 640, 640),
)
WIDTHS = (QKVP, DP, 2 * FF, FF)
N_AG = 19
N_RS = 12


def permutation():
    table = np.zeros((D, DP), np.float32)
    for d in range(D):
        f, r = divmod(d, ROWS)
        y, z, x = f // 8, (f // 2) % 4, f % 2
        h, rr = divmod(r, 16)
        at = (z * 2 + x) * 4 + y if h == 0 else (y * 2 + x) * 4 + z
        table[d, h * HALF + at * 16 + rr] = 1.0
    return table


def lane_frequencies():
    i = np.arange(128) % 32
    return np.power(np.float32(BASE), -(i.astype(np.float32)) * np.float32(2.0 / HEAD))[None, :].astype(np.float32)


def nn(a, b):
    return lax.dot_general(a, b, (((1,), (0,)), ((), ())), preferred_element_type=F32)


def nt(a, b):
    return lax.dot_general(a, b, (((1,), (1,)), ((), ())), preferred_element_type=F32)


def tn(a, b):
    return lax.dot_general(a, b, (((0,), (0,)), ((), ())), preferred_element_type=F32)


def over(total, tile, body):
    whole = total // tile

    @pl.loop(0, whole)
    def _(i):
        body(pl.ds(pl.multiple_of(i * tile, tile), tile))

    if total % tile:
        body(pl.ds(whole * tile, total % tile))


def kernel(
    tok, seg, ga, wq_in, wo_in, gf, wg_in, wd_in, dout, perm_in, freq,
    acts, igrad, gga, ggf, *rest,
):
    n = len(PIECES)
    ns = len(SUMS)
    fin, rest = rest[:ns], rest[ns:]
    (wq, wo, wg, wd), rest = rest[:4], rest[4:]
    shards, rest = rest[:4], rest[4:]
    (pq, po, pg, pd), rest = rest[:4], rest[4:]
    rb, ra, rx, r3 = (rest[k * ns:(k + 1) * ns] for k in range(4))
    rest = rest[4 * ns:]
    lts, rest = rest[:4], rest[4:]
    (
        perm, raw, draw, xin, din, act, ig, a960, i960,
        qkv, qk, vv, pf, o, h, xn1, xn2, gate, up, mm,
        dgu, dh, da, do, dps, dsb, dqkf, dqkv, cosr, sinr, gains,
        in_s, ag_s, ag_r, rs_s, rs_r, mi_s, mi_r,
    ) = rest
    weights = (wq, wo, wg, wd)

    sec = lax.axis_index("section")
    f = lax.axis_index("fsdp")
    c = lax.axis_index("ctx")
    y = f // 8
    z = lax.rem(f // 2, 4)
    x = lax.rem(f, 2)
    a = y + c * (z - y)
    cc = z + c * (y - z)
    other_x = 1 - x

    def at(a_, x_, cc_):
        yy = a_ + c * (cc_ - a_)
        zz = cc_ + c * (a_ - cc_)
        return (sec, (yy * 4 + zz) * 2 + x_, c)

    def mod4(v):
        return lax.rem(v + 4, 4)

    def row(cc_, x_, a_, half=None):
        half = c if half is None else half
        return pl.multiple_of(half * HALF + ((cc_ * 2 + x_) * 4 + a_) * 16, 16)

    own_half = pl.ds(pl.multiple_of(64 * c, 64), 64)
    sib_half = pl.ds(pl.multiple_of(64 * (1 - c), 64), 64)
    own16 = pl.ds(pl.multiple_of(16 * c, 16), 16)
    fetch = [
        pltpu.make_async_copy(src, dst, in_s.at[k])
        for k, (src, dst) in enumerate((
            (wq_in, shards[0]), (wo_in, shards[1]), (wg_in, shards[2]), (wd_in, shards[3]),
            (tok.at[c], raw.at[own_half]), (dout.at[c], draw.at[own_half]), (perm_in, perm),
        ))
    ]
    for copy in fetch:
        copy.start()

    sibling = (sec, f, 1 - c)
    partner = (1 - sec, f, c)
    last_up, last_down = at(a, x, mod4(cc + 1)), at(a, x, mod4(cc + 3))
    over_x = at(a, other_x, cc)
    first_to = [at(mod4(a + step), x, cc) for step in (1, 3, 2)]

    barrier = pltpu.get_barrier_semaphore()
    friends = first_to + [over_x, last_up, last_down, sibling, partner]
    for dev in friends:
        pl.semaphore_signal(barrier, inc=1, device_id=dev, device_id_type=MESH)

    gains[...] = jnp.zeros_like(gains)
    gains[0:1, 0:ROWS] = ga[...].astype(F32)
    gains[1:2, 0:ROWS] = gf[...].astype(F32)
    gain_cols = gains[0:8, 0:128].T
    pl.semaphore_wait(barrier, len(friends))

    def remote(src, dst, ssem, rsem, dev):
        return pltpu.make_async_remote_copy(
            src_ref=src, dst_ref=dst, send_sem=ssem, recv_sem=rsem, device_id=dev, device_id_type=MESH
        )

    own_cols = [pl.ds(256 * k, 256) for k in range(4)]
    single = (
        [(tok.at[1 - c], raw.at[own_half], sibling), (dout.at[1 - c], draw.at[own_half], sibling)]
        + [(act.at[:, cols], xin.at[:, cols], partner) for cols in own_cols]
        + [(ig, din, partner), (a960.at[sib_half], acts.at[c], sibling), (i960.at[sib_half], igrad.at[c], sibling)]
    )

    def one(k):
        src, dst, dev = single[k]
        return remote(src, dst, mi_s.at[k], mi_r.at[k], dev)

    steps4 = range(4)
    xs = (x, other_x)
    mine = {(d, s): row(mod4(cc + d), xs[s], 0) for d in steps4 for s in range(2)}
    theirs = {(d, s): row(mod4(a + d), xs[s], 0, 1 - c) for d in steps4 for s in range(2)}
    slab = [row(cc, x, mod4(a + d)) for d in steps4]
    ag_table = [
        (slab[0], slab[3], 16, first_to[0]),
        (slab[0], slab[1], 16, first_to[1]),
        (slab[0], slab[2], 16, first_to[2]),
        (mine[0, 0], mine[0, 1], 64, over_x),
        (mine[0, 0], mine[3, 0], 64, last_up),
        (mine[0, 0], mine[1, 0], 64, last_down),
        (mine[0, 1], mine[3, 1], 64, last_up),
        (mine[0, 1], mine[1, 1], 64, last_down),
        (mine[3, 0], mine[2, 0], 64, last_up),
        (mine[1, 1], mine[2, 1], 64, last_down),
    ] + [
        (mine[key], theirs[key], 64, sibling)
        for key in ((0, 0), (0, 1), (3, 0), (1, 0), (3, 1), (1, 1), (2, 0), (2, 1))
    ]

    ag_table.append((mine[2, 0], mine[2, 1], 64, over_x))
    ag_parts = {
        8: (pl.multiple_of(mine[3, 0], 32), pl.multiple_of(mine[2, 0], 32), 32, last_up),
        9: (pl.multiple_of(mine[1, 0] + 32, 32), pl.multiple_of(mine[2, 0] + 32, 32), 32, last_down),
    }

    def ag_copy(m, k, arriving=False):
        w, first, cols, wide = PIECES[m]
        source, landing, rows, dev = ag_parts[k] if wide and k in ag_parts else ag_table[k]
        piece = weights[w].at[pl.ds(landing if arriving else source, rows), pl.ds(first, cols)]
        return remote(piece, piece, ag_s.at[m * N_AG + k], ag_r.at[m * N_AG + k], dev)

    def ag_send(m, *ks):
        for k in ks:
            ag_copy(m, k).start()

    def ag_wait(m, *ks):
        for k in ks:
            ag_copy(m, k, True).wait_recv()

    def ag1(m):
        ag_wait(m, 0, 1, 2)
        ag_send(m, 4, 5, 3, 10)

    def ag2(m):
        ag_wait(m, 3)
        ag_send(m, 6, 7, 11)
        ag_wait(m, 4)
        ag_send(m, 8, 12)
        ag_wait(m, 5)
        if PIECES[m][3]:
            ag_send(m, 9)
        ag_send(m, 13)

    def ag3(m):
        ag_wait(m, 7)
        if not PIECES[m][3]:
            ag_send(m, 9)
        ag_send(m, 15)
        ag_wait(m, 6)
        ag_send(m, 14)

    def ag4(m):
        if PIECES[m][3]:
            ag_wait(m, 8, 9)
            ag_send(m, 18, 16)
        else:
            ag_wait(m, 8)
            ag_send(m, 16)
            ag_wait(m, 9)
            ag_send(m, 17)

    def ag5(m):
        if PIECES[m][3]:
            ag_wait(m, 18)
            ag_send(m, 17)

    def ag6(m):
        ag_wait(m, *range(10, 18))

    ag_steps = n + 6

    def ag_step(t):
        for stage, late in ((ag1, 0), (ag2, 2), (ag3, 3), (ag4, 4), (ag5, 5), (ag6, 6)):
            if 0 <= t - late < n:
                stage(t - late)

    def ag_drain():
        for m in range(n):
            for k in range(N_AG if PIECES[m][3] else N_AG - 1):
                ag_copy(m, k).wait_send()

    one(0).start()
    for w, (pack, cols) in enumerate(((pq, QKV), (po, D), (pg, 2 * FF), (pd, FF))):
        if cols < pack.shape[1]:
            pack[:, cols:] = jnp.zeros((32, pack.shape[1] - cols), BF)
        pack[16:32, :] = jnp.zeros((16, pack.shape[1]), BF)
        fetch[w].wait()
        pack[0:ROWS, 0:cols] = shards[w][...]
        if w == 0:
            pack[:, QKV:QKV + 2] = gain_cols[0:32, 0:2].astype(BF)
        weights[w][pl.ds(slab[0], 16), :] = pack[own16, :]
        for m in range(n):
            if PIECES[m][0] == w:
                ag_send(m, 0, 1, 2)
    one(1).start()

    places = lax.broadcasted_iota(jnp.int32, (SEQ, SEQ), 0)
    lanes = lax.broadcasted_iota(jnp.int32, (SEQ, SEQ), 1)
    key_seg = jnp.broadcast_to(seg[pl.ds(c, 1), :].astype(F32), (SEQ, SEQ))
    query_seg = key_seg.T
    allowed = (key_seg == query_seg) & (lanes <= places)
    earlier = jnp.sum(jnp.where(key_seg < query_seg, 1.0, 0.0), axis=1, keepdims=True)
    pos = places.astype(F32) - earlier
    angle = pos * freq[...]
    first_half = lax.rem(lanes, HEAD) < HEAD // 2
    cosr[...] = jnp.cos(angle)
    sinr[...] = jnp.where(first_half, -jnp.sin(angle), jnp.sin(angle))

    def swap(u):
        return jnp.where(first_half, pltpu.roll(u, 96, 1), pltpu.roll(u, 32, 1))

    ag_step(0)
    for copy in fetch[4:]:
        copy.wait()
    for k in range(2):
        src, _, dev = single[k]
        remote(src, (raw, draw)[k].at[sib_half], mi_s.at[k], mi_r.at[k], dev).wait_recv()

    @pl.when(sec == 0)
    def _():
        xin[...] = nn(raw[...], perm[...]).astype(BF)

    @pl.when(sec == 1)
    def _():
        din[...] = nn(draw[...], perm[...]).astype(BF)

    def ag_first(*ts):
        @pl.when(sec == 0)
        def _():
            for t in ts:
                ag_step(t)

    @pl.when(sec == 1)
    def _():
        for t in range(1, ag_steps):
            ag_step(t)
        ag_drain()
        for k in range(2, 6):
            one(k).wait_recv()

    ag_first(1, 2, 3, 4, 5, 6)

    def norm(v):
        inverse = lax.rsqrt(jnp.sum(v * v, axis=1, keepdims=True) * (1.0 / D) + EPS)
        return v * inverse, inverse

    def norm_back(d, normal, inverse):
        return inverse * (d - normal * (jnp.sum(normal * d, axis=1, keepdims=True) * (1.0 / D)))

    gains[...] = wq[:, 1536:1664].astype(F32).T[64:72, :]
    xhat, _ = norm(xin[...].astype(F32))
    xn1[...] = (xhat * gains[0:1, :]).astype(BF)
    qkv[...] = nn(xn1[...], wq[...])
    for t in range(QK // 128):
        cols = pl.ds(128 * t, 128)
        u = qkv[:, cols]
        qk[:, cols] = (u * cosr[...] + swap(u) * sinr[...]).astype(BF)
    vv[...] = qkv[:, QK:QKVP].astype(BF)
    ag_first(7)
    group = HEADS // KV_HEADS

    def head(hd):
        return slice(HEAD * hd, HEAD * (hd + 1))

    def key_of(hd):
        return qk[:, head(HEADS + hd // group)]

    def value_of(hd):
        return vv[:, head(hd // group)]

    scale = HEAD ** -0.5
    for hd in range(HEADS):
        pf[hd] = nt(qk[:, head(hd)], key_of(hd))
    for hd in range(HEADS):
        s = jnp.where(allowed, pf[hd] * scale, -1e30)
        e = jnp.exp(s - jnp.max(s, axis=1, keepdims=True))
        pf[hd] = e / jnp.sum(e, axis=1, keepdims=True)
    ag_first(8)
    o[:, HEADS * HEAD:] = jnp.zeros((SEQ, DP - HEADS * HEAD), BF)
    for hd in range(HEADS):
        o[:, head(hd)] = nn(pf[hd].astype(BF), value_of(hd)).astype(BF)
    h[...] = xin[...].astype(F32) + nt(o[...], wo[...])
    xhat, _ = norm(h[...])
    xn2[...] = (xhat * gains[1:2, :]).astype(BF)
    ag_first(9)

    def gated(j):
        cols = pl.ds(PART * j, PART)
        gate[:, cols] = nn(xn2[...], wg[:, cols])
        up[:, cols] = nn(xn2[...], wg[:, pl.ds(FF + PART * j, PART)])
        g_ = gate[:, cols]
        mm[:, cols] = (g_ * jax.nn.sigmoid(g_) * up[:, cols]).astype(BF)

    gated(0)
    ag_first(10, 11)
    gated(1)
    ag_first(12)
    dh[...] = h[...] + nt(mm[:, 0:PART], wd[:, 0:PART])
    ag_first(13)
    for k, cols in enumerate(own_cols):
        act[:, cols] = (dh[:, cols] + nt(mm[:, PART:], wd[cols, PART:])).astype(BF)

        @pl.when(sec == 0)
        def _():
            one(2 + k).start()

    @pl.when(sec == 0)
    def _():
        ag_drain()
        for k in range(2, 6):
            one(k).wait_send()
        one(6).wait_recv()

    pairs = ((xn1, dqkv), (da, o), (xn2, dgu), (din, mm))
    lower = pl.multiple_of(c * HALF, HALF)
    upper = pl.multiple_of((1 - c) * HALF, HALF)
    rs_table = (
        (upper, HALF, sibling), (mine[2, 0], 64, last_up), (mine[2, 1], 64, last_down), (mine[1, 1], 64, last_up),
        (mine[3, 0], 64, last_down), (mine[1, 0], 64, last_up), (mine[3, 1], 64, last_down), (mine[0, 1], 64, over_x),
        (slab[1], 16, first_to[0]), (slab[3], 16, first_to[1]), (slab[2], 16, first_to[2]),
    )

    def rs_copy(m, k):
        w, first, cols = SUMS[m]
        sems = rs_s.at[m * N_RS + k], rs_r.at[m * N_RS + k]
        if k == 11:
            piece = fin[m].at[own16]
            return remote(piece, piece, *sems, sibling)
        start, rows, dev = rs_table[k]
        if k == 0:
            dst = rb[m]
        elif k < 7:
            dst = ra[m].at[pl.ds(64 * (k - 1), rows)]
        elif k == 7:
            dst = rx[m]
        else:
            dst = r3[m].at[pl.ds(16 * (k - 8), 16)]
        return remote(weights[w].at[pl.ds(start, rows), pl.ds(first, cols)], dst, *sems, dev)

    def rs_send(m, *ks):
        for k in ks:
            rs_copy(m, k).start()

    def rs_wait(m, *ks):
        for k in ks:
            rs_copy(m, k).wait_recv()

    def add_in(m, start, rows, source, source_row):
        w, first, cols = SUMS[m]
        ref = weights[w]
        width = 640 if cols % 640 == 0 else 512

        def body(tile):
            there = pl.ds(pl.multiple_of(tile.start + first, 128), tile.size)
            ref[pl.ds(start, rows), there] = ref[pl.ds(start, rows), there] + source[pl.ds(source_row, rows), tile]

        over(cols, width, body)

    def rs0(m):
        w, first, cols = SUMS[m]
        left, right = pairs[w]
        if first == 0:
            lts[w][...] = left[...].T

        def body(tile):
            there = pl.ds(pl.multiple_of(tile.start + first, 128), tile.size)
            for r in range(4):
                rows = pl.ds(256 * r, 256)
                weights[w][rows, there] = nn(lts[w][rows, :], right[:, there]).astype(BF)

        over(cols, 256, body)
        rs_send(m, 0)

    def rs1(m):
        rs_wait(m, 0)
        add_in(m, lower, HALF, rb[m], 0)
        rs_send(m, 1, 2, 3, 4)

    def rs2(m):
        for k, into in ((1, mine[1, 0]), (2, mine[3, 1])):
            rs_wait(m, k)
            add_in(m, into, 64, ra[m], 64 * (k - 1))
            rs_send(m, k + 4)

    def rs3(m):
        for k, s in ((3, 1), (4, 0), (5, 0), (6, 1)):
            rs_wait(m, k)
            add_in(m, mine[0, s], 64, ra[m], 64 * (k - 1))
        rs_send(m, 7)

    def rs4(m):
        rs_wait(m, 7)
        add_in(m, mine[0, 0], 64, rx[m], 0)
        rs_send(m, 8, 9, 10)

    def rs5(m):
        w, first, cols = SUMS[m]
        rs_wait(m, 8, 9, 10)
        total = weights[w][pl.ds(slab[0], 16), pl.ds(first, cols)].astype(F32)
        for k in range(3):
            total = total + r3[m][pl.ds(16 * k, 16), :].astype(F32)
        fin[m][own16, :] = total
        rs_send(m, 11)

    def rs6(m):
        remote(fin[m].at[own16], fin[m].at[pl.ds(pl.multiple_of(16 * (1 - c), 16), 16)],
               rs_s.at[m * N_RS + 11], rs_r.at[m * N_RS + 11], sibling).wait_recv()
        for k in range(N_RS):
            rs_copy(m, k).wait_send()

    rs_order = ((rs0, 0), (rs1, 1), (rs2, 2), (rs3, 3), (rs4, 5), (rs5, 7), (rs6, 9))
    rs_steps = ns + 9

    def reduce(*ts):
        for t in ts:
            for stage, late in rs_order:
                if 0 <= t - late < ns:
                    stage(t - late)

    def reduce_first(*ts):
        @pl.when(sec == 0)
        def _():
            reduce(*ts)

    for j in range(2):
        cols = pl.ds(PART * j, PART)
        dm = nn(din[...], wd[:, cols])
        g_ = gate[:, cols]
        sg = jax.nn.sigmoid(g_)
        dgu[:, cols] = (dm * up[:, cols] * sg * (1.0 + g_ * (1.0 - sg))).astype(BF)
        dgu[:, pl.ds(FF + PART * j, PART)] = (dm * g_ * sg).astype(BF)
    reduce_first(0)
    dh[...] = nt(dgu[...], wg[...])
    reduce_first(1)
    xhat, inv = norm(h[...])
    dhv = din[...].astype(F32) + norm_back(dh[...] * gains[1:2, :], xhat, inv)
    dh[...] = dhv
    da[...] = dhv.astype(BF)
    do[...] = nn(da[...], wo[...]).astype(BF)
    reduce_first(2)
    for hd in range(HEADS):
        dps[hd] = nt(do[:, head(hd)], value_of(hd))
    for hd in range(HEADS):
        p, dp = pf[hd], dps[hd]
        dsb[hd] = (p * (dp - jnp.sum(dp * p, axis=1, keepdims=True))).astype(BF)
    reduce_first(3)
    dqkv[:, QKV:] = jnp.zeros((SEQ, QKVP - QKV), BF)
    for hd in range(HEADS):
        dqkf[:, head(hd)] = nn(dsb[hd], key_of(hd)) * scale
    for g in range(KV_HEADS):
        hds = range(group * g, group * (g + 1))
        dqkf[:, head(HEADS + g)] = sum(tn(dsb[hd], qk[:, head(hd)]) for hd in hds) * scale
        dv = sum(tn(pf[hd].astype(BF), do[:, head(hd)]) for hd in hds)
        dqkv[:, QK + HEAD * g:QK + HEAD * (g + 1)] = dv.astype(BF)
    reduce_first(4)
    for t in range(QK // 128):
        cols = pl.ds(128 * t, 128)
        u = dqkf[:, cols]
        dqkv[:, cols] = (u * cosr[...] - swap(u) * sinr[...]).astype(BF)
    h[...] = nt(dqkv[...], wq[...])
    reduce_first(5)
    xhat, inv = norm(xin[...].astype(F32))
    ig[...] = (dh[...] + norm_back(h[...] * gains[0:1, :], xhat, inv)).astype(BF)

    @pl.when(sec == 1)
    def _():
        one(6).start()
        reduce(0, 1, 2, 3, 4, 5)

    reduce(6, 7, 8, 9)
    a960[...] = nt(act[...], perm[...]).astype(BF)
    acts[c] = a960[own_half, :]
    one(7).start()
    i960[...] = nt(ig[...], perm[...]).astype(BF)
    igrad[c] = i960[own_half, :]
    one(8).start()
    reduce(10, 11, 12)
    for k in (7, 8):
        src, dst, dev = single[k]
        remote(src, (acts, igrad)[k - 7].at[1 - c], mi_s.at[k], mi_r.at[k], dev).wait_recv()
        one(k).wait_send()

    @pl.when(sec == 1)
    def _():
        one(6).wait_send()

    one(0).wait_send()
    one(1).wait_send()
    reduce(*range(13, rs_steps - 2))

    sums = [0.0] * 4
    for m, (w, first, cols) in enumerate(SUMS):
        if w in (0, 2):
            cols = min(cols, (QKV, D, 2 * FF, FF)[w])
            shard = (pq, po, pg, pd)[w][:, first:first + cols].astype(F32)
            sums[w] = sums[w] + jnp.sum(fin[m][:, 0:cols] * shard, axis=1, keepdims=True)
    gga[...] = jnp.broadcast_to(sums[0], (32, 128)).T[0:1, 0:ROWS] / ga[...].astype(F32)
    ggf[...] = jnp.broadcast_to(sums[2], (32, 128)).T[0:1, 0:ROWS] / gf[...].astype(F32)
    reduce(rs_steps - 2, rs_steps - 1)


def lay_out(*refs):
    n = len(SUMS)
    passed, fin, rest = refs[:4], refs[4:4 + n], refs[4 + n:]
    acts, igrad, gga, ggf, gq, go, gg, gd = rest
    for source, target in zip(passed, (acts, igrad, gga, ggf)):
        target[...] = source[...]
    targets = (gq, go, gg, gd)
    for m, (w, first, cols) in enumerate(SUMS):
        cols = min(cols, (QKV, D, 2 * FF, FF)[w])
        targets[w][:, 0, first:first + cols] = fin[m][0:ROWS, 0:cols]


def per_device(tokens, segments, gain_attn, w_qkv, w_out, gain_ffn, w_gu, w_down, d_out):
    n, ns = len(PIECES), len(SUMS)
    vmem = pl.BlockSpec(memory_space=pltpu.VMEM)
    per_sum = lambda rows: [pltpu.VMEM((rows, cols), BF) for _, _, cols in SUMS]
    scratch = (
        [pltpu.VMEM((DP, w), BF) for w in WIDTHS]
        + [pltpu.VMEM((ROWS, w), BF) for w in (QKV, D, 2 * FF, FF)]
        + [pltpu.VMEM((32, w), BF) for w in WIDTHS]
        + per_sum(HALF) + per_sum(384) + per_sum(64) + per_sum(48)
        + [pltpu.VMEM((DP, SEQ), BF)] * 4
        + [
            pltpu.VMEM((D, DP), BF),
            pltpu.VMEM((SEQ, D), BF), pltpu.VMEM((SEQ, D), BF),
            pltpu.VMEM((SEQ, DP), BF), pltpu.VMEM((SEQ, DP), BF),
            pltpu.VMEM((SEQ, DP), BF), pltpu.VMEM((SEQ, DP), BF),
            pltpu.VMEM((SEQ, D), BF), pltpu.VMEM((SEQ, D), BF),
            pltpu.VMEM((SEQ, QKVP), F32), pltpu.VMEM((SEQ, QK), BF), pltpu.VMEM((SEQ, QKVP - QK), BF),
            pltpu.VMEM((HEADS, SEQ, SEQ), F32), pltpu.VMEM((SEQ, DP), BF), pltpu.VMEM((SEQ, DP), F32),
            pltpu.VMEM((SEQ, DP), BF), pltpu.VMEM((SEQ, DP), BF),
            pltpu.VMEM((SEQ, FF), F32), pltpu.VMEM((SEQ, FF), F32), pltpu.VMEM((SEQ, FF), BF),
            pltpu.VMEM((SEQ, 2 * FF), BF), pltpu.VMEM((SEQ, DP), F32),
            pltpu.VMEM((SEQ, DP), BF), pltpu.VMEM((SEQ, DP), BF),
            pltpu.VMEM((HEADS, SEQ, SEQ), F32), pltpu.VMEM((HEADS, SEQ, SEQ), BF),
            pltpu.VMEM((SEQ, QK), F32), pltpu.VMEM((SEQ, QKVP), BF),
            pltpu.VMEM((SEQ, SEQ), F32), pltpu.VMEM((SEQ, SEQ), F32), pltpu.VMEM((8, DP), F32),
        ]
        + [pltpu.SemaphoreType.DMA((7,))]
        + [pltpu.SemaphoreType.DMA((n * N_AG,))] * 2
        + [pltpu.SemaphoreType.DMA((ns * N_RS,))] * 2
        + [pltpu.SemaphoreType.DMA((9,))] * 2
    )
    shape = jax.ShapeDtypeStruct
    hbm = pl.BlockSpec(memory_space=pl.ANY)
    passed = (shape(tokens.shape, BF), shape(tokens.shape, BF), shape((1, ROWS), F32), shape((1, ROWS), F32))
    out = pl.pallas_call(
        kernel,
        out_shape=passed + tuple(shape((32, cols), F32) for _, _, cols in SUMS),
        in_specs=[hbm, vmem, vmem, hbm, hbm, vmem, hbm, hbm, hbm, hbm, vmem],
        out_specs=(vmem,) * (4 + ns),
        scratch_shapes=scratch,
        compiler_params=pltpu.CompilerParams(
            collective_id=0, has_side_effects=True, vmem_limit_bytes=63 * 1024 * 1024
        ),
    )(
        tokens, segments, gain_attn, w_qkv[0], w_out[0], gain_ffn, w_gu[0], w_down[0], d_out,
        jnp.asarray(permutation(), BF), jnp.asarray(lane_frequencies(), F32),
    )
    acts, igrad, gga, ggf, gq, go, gg, gd = pl.pallas_call(
        lay_out,
        out_shape=passed + tuple(shape((ROWS, 1, cols), F32) for cols in (QKV, D, 2 * FF, FF)),
        in_specs=[vmem] * (4 + ns),
        out_specs=(vmem,) * 8,
    )(*out)
    gq, go, gg, gd = (jnp.swapaxes(g, 0, 1) for g in (gq, go, gg, gd))
    return acts[None], igrad[None], gga, gq, go, ggf, gg, gd


def solution(mesh):
    in_specs = (
        P(None, ("fsdp", "ctx"), None),
        P(None, "fsdp"),
        P("section", "fsdp"),
        P("section", "fsdp", None),
        P("section", "fsdp", None),
        P("section", "fsdp"),
        P("section", "fsdp", None),
        P("section", "fsdp", None),
        P(None, ("fsdp", "ctx"), None),
    )
    out_specs = (
        P("section", None, ("fsdp", "ctx"), None),
        P("section", None, ("fsdp", "ctx"), None),
        P("section", "fsdp"),
        P("section", "fsdp", None),
        P("section", "fsdp", None),
        P("section", "fsdp"),
        P("section", "fsdp", None),
        P("section", "fsdp", None),
    )
    return jax.shard_map(
        per_device, mesh=mesh, in_specs=in_specs, out_specs=out_specs, check_vma=False
    )
```

```python
import functools

import jax
import jax.numpy as jnp
import numpy as np
from jax import lax
from jax.experimental import pallas as pl
from jax.experimental.pallas import tpu as pltpu
from jax.sharding import PartitionSpec as P

D = 960
HEADS = 15
KV_HEADS = 5
HEAD = 64
FF = 2560
SEQ = 128
EPS = 1e-05
BASE = 100000.0

DP = 1024
HALF = DP // 2
QKV = 1600
QKVP = 1664
QK = 1280
ROWS = 30
BF = jnp.bfloat16
F32 = jnp.float32
MESH = pl.DeviceIdType.MESH

PART = FF // 2
PIECES = (
    (0, 0, QKVP, 1), (1, 0, DP, 0), (2, 0, PART, 1), (2, FF, PART, 0), (2, PART, PART, 1), (2, FF + PART, PART, 0),
    (3, 0, PART, 0), (3, PART, PART, 0),
)
SUMS = (
    (3, 0, 640), (3, 640, 640), (2, 0, PART), (2, FF, PART), (2, PART, PART), (2, FF + PART, PART), (1, 0, DP), (0, 0, QKVP),
    (3, PART, 640), (3, PART + 640, 640),
)
WIDTHS = (QKVP, DP, 2 * FF, FF)
N_AG = 19
N_RS = 16


def permutation():
    table = np.zeros((D, DP), np.float32)
    for d in range(D):
        f, r = divmod(d, ROWS)
        y, z, x = f // 8, (f // 2) % 4, f % 2
        h, rr = divmod(r, 16)
        at = (z * 2 + x) * 4 + y if h == 0 else (y * 2 + x) * 4 + z
        table[d, h * HALF + at * 16 + rr] = 1.0
    return table


def lane_frequencies():
    i = np.arange(128) % 32
    return np.power(np.float32(BASE), -(i.astype(np.float32)) * np.float32(2.0 / HEAD))[None, :].astype(np.float32)


def nn(a, b):
    return lax.dot_general(a, b, (((1,), (0,)), ((), ())), preferred_element_type=F32)


def nt(a, b):
    return lax.dot_general(a, b, (((1,), (1,)), ((), ())), preferred_element_type=F32)


def tn(a, b):
    return lax.dot_general(a, b, (((0,), (0,)), ((), ())), preferred_element_type=F32)


def over(total, tile, body):
    whole = total // tile

    @pl.loop(0, whole)
    def _(i):
        body(pl.ds(pl.multiple_of(i * tile, tile), tile))

    if total % tile:
        body(pl.ds(whole * tile, total % tile))


def kernel(
    tok, seg, ga, wq_in, wo_in, gf, wg_in, wd_in, dout, perm_in, freq,
    acts, igrad, gga, ggf, *rest,
):
    n = len(PIECES)
    ns = len(SUMS)
    fin, rest = rest[:ns], rest[ns:]
    (wq, wo, wg, wd), rest = rest[:4], rest[4:]
    shards, rest = rest[:4], rest[4:]
    (pq, po, pg, pd), rest = rest[:4], rest[4:]
    rb, ra, rx, r3 = (rest[k * ns:(k + 1) * ns] for k in range(4))
    rest = rest[4 * ns:]
    lts, rest = rest[:4], rest[4:]
    (
        perm, raw, draw, xin, din, act, ig, a960, i960,
        qkv, qk, vv, pf, o, h, xn1, xn2, gate, up, mm,
        dgu, dh, da, do, dps, dsb, dqkf, dqkv, cosr, sinr, gains,
        in_s, ag_s, ag_r, rs_s, rs_r, mi_s, mi_r,
    ) = rest
    weights = (wq, wo, wg, wd)

    sec = lax.axis_index("section")
    f = lax.axis_index("fsdp")
    c = lax.axis_index("ctx")
    y = f // 8
    z = lax.rem(f // 2, 4)
    x = lax.rem(f, 2)
    a = y + c * (z - y)
    cc = z + c * (y - z)
    other_x = 1 - x

    def at(a_, x_, cc_):
        yy = a_ + c * (cc_ - a_)
        zz = cc_ + c * (a_ - cc_)
        return (sec, (yy * 4 + zz) * 2 + x_, c)

    def mod4(v):
        return lax.rem(v + 4, 4)

    def row(cc_, x_, a_, half=None):
        half = c if half is None else half
        return pl.multiple_of(half * HALF + ((cc_ * 2 + x_) * 4 + a_) * 16, 16)

    own_half = pl.ds(pl.multiple_of(64 * c, 64), 64)
    sib_half = pl.ds(pl.multiple_of(64 * (1 - c), 64), 64)
    own16 = pl.ds(pl.multiple_of(16 * c, 16), 16)
    fetch = [
        pltpu.make_async_copy(src, dst, in_s.at[k])
        for k, (src, dst) in enumerate((
            (wq_in, shards[0]), (wo_in, shards[1]), (wg_in, shards[2]), (wd_in, shards[3]),
            (tok.at[c], raw.at[own_half]), (dout.at[c], draw.at[own_half]), (perm_in, perm),
        ))
    ]
    for copy in fetch:
        copy.start()

    sibling = (sec, f, 1 - c)
    partner = (1 - sec, f, c)
    last_up, last_down = at(a, x, mod4(cc + 1)), at(a, x, mod4(cc + 3))
    over_x = at(a, other_x, cc)
    first_to = [at(mod4(a + step), x, cc) for step in (1, 3, 2)]
    last_far = at(a, x, mod4(cc + 2))
    across = [at(mod4(a + step), other_x, cc) for step in range(4)]

    barrier = pltpu.get_barrier_semaphore()
    friends = first_to + across + [last_up, last_down, last_far, sibling, partner]
    for dev in friends:
        pl.semaphore_signal(barrier, inc=1, device_id=dev, device_id_type=MESH)

    gains[...] = jnp.zeros_like(gains)
    gains[0:1, 0:ROWS] = ga[...].astype(F32)
    gains[1:2, 0:ROWS] = gf[...].astype(F32)
    gain_cols = gains[0:8, 0:128].T
    pl.semaphore_wait(barrier, len(friends))

    def remote(src, dst, ssem, rsem, dev):
        return pltpu.make_async_remote_copy(
            src_ref=src, dst_ref=dst, send_sem=ssem, recv_sem=rsem, device_id=dev, device_id_type=MESH
        )

    own_cols = [pl.ds(256 * k, 256) for k in range(4)]
    single = (
        [(tok.at[1 - c], raw.at[own_half], sibling), (dout.at[1 - c], draw.at[own_half], sibling)]
        + [(act.at[:, cols], xin.at[:, cols], partner) for cols in own_cols]
        + [(ig, din, partner), (a960.at[sib_half], acts.at[c], sibling), (i960.at[sib_half], igrad.at[c], sibling)]
    )

    def one(k):
        src, dst, dev = single[k]
        return remote(src, dst, mi_s.at[k], mi_r.at[k], dev)

    steps4 = range(4)
    xs = (x, other_x)
    mine = {(d, s): row(mod4(cc + d), xs[s], 0) for d in steps4 for s in range(2)}
    theirs = {(d, s): row(mod4(a + d), xs[s], 0, 1 - c) for d in steps4 for s in range(2)}
    slab = [row(cc, x, mod4(a + d)) for d in steps4]
    ag_table = [
        (slab[0], slab[3], 16, first_to[0]),
        (slab[0], slab[1], 16, first_to[1]),
        (slab[0], slab[2], 16, first_to[2]),
        (mine[0, 0], mine[0, 1], 64, over_x),
        (mine[0, 0], mine[3, 0], 64, last_up),
        (mine[0, 0], mine[1, 0], 64, last_down),
        (mine[0, 1], mine[3, 1], 64, last_up),
        (mine[0, 1], mine[1, 1], 64, last_down),
        (mine[3, 0], mine[2, 0], 64, last_up),
        (mine[1, 1], mine[2, 1], 64, last_down),
    ] + [
        (mine[key], theirs[key], 64, sibling)
        for key in ((0, 0), (0, 1), (3, 0), (1, 0), (3, 1), (1, 1), (2, 0), (2, 1))
    ]

    ag_table.append((mine[2, 0], mine[2, 1], 64, over_x))
    ag_parts = {
        8: (pl.multiple_of(mine[3, 0], 32), pl.multiple_of(mine[2, 0], 32), 32, last_up),
        9: (pl.multiple_of(mine[1, 0] + 32, 32), pl.multiple_of(mine[2, 0] + 32, 32), 32, last_down),
    }

    def ag_copy(m, k, arriving=False):
        w, first, cols, wide = PIECES[m]
        source, landing, rows, dev = ag_parts[k] if wide and k in ag_parts else ag_table[k]
        piece = weights[w].at[pl.ds(landing if arriving else source, rows), pl.ds(first, cols)]
        return remote(piece, piece, ag_s.at[m * N_AG + k], ag_r.at[m * N_AG + k], dev)

    def ag_send(m, *ks):
        for k in ks:
            ag_copy(m, k).start()

    def ag_wait(m, *ks):
        for k in ks:
            ag_copy(m, k, True).wait_recv()

    def ag1(m):
        ag_wait(m, 0, 1, 2)
        ag_send(m, 4, 5, 3, 10)

    def ag2(m):
        ag_wait(m, 3)
        ag_send(m, 6, 7, 11)
        ag_wait(m, 4)
        ag_send(m, 8, 12)
        ag_wait(m, 5)
        if PIECES[m][3]:
            ag_send(m, 9)
        ag_send(m, 13)

    def ag3(m):
        ag_wait(m, 7)
        if not PIECES[m][3]:
            ag_send(m, 9)
        ag_send(m, 15)
        ag_wait(m, 6)
        ag_send(m, 14)

    def ag4(m):
        if PIECES[m][3]:
            ag_wait(m, 8, 9)
            ag_send(m, 18, 16)
        else:
            ag_wait(m, 8)
            ag_send(m, 16)
            ag_wait(m, 9)
            ag_send(m, 17)

    def ag5(m):
        if PIECES[m][3]:
            ag_wait(m, 18)
            ag_send(m, 17)

    def ag6(m):
        ag_wait(m, *range(10, 18))

    ag_steps = n + 6

    def ag_step(t):
        for stage, late in ((ag1, 0), (ag2, 2), (ag3, 3), (ag4, 4), (ag5, 5), (ag6, 6)):
            if 0 <= t - late < n:
                stage(t - late)

    def ag_drain():
        for m in range(n):
            for k in range(N_AG if PIECES[m][3] else N_AG - 1):
                ag_copy(m, k).wait_send()

    one(0).start()
    for w, (pack, cols) in enumerate(((pq, QKV), (po, D), (pg, 2 * FF), (pd, FF))):
        if cols < pack.shape[1]:
            pack[:, cols:] = jnp.zeros((32, pack.shape[1] - cols), BF)
        pack[16:32, :] = jnp.zeros((16, pack.shape[1]), BF)
        fetch[w].wait()
        pack[0:ROWS, 0:cols] = shards[w][...]
        if w == 0:
            pack[:, QKV:QKV + 2] = gain_cols[0:32, 0:2].astype(BF)
        weights[w][pl.ds(slab[0], 16), :] = pack[own16, :]
        for m in range(n):
            if PIECES[m][0] == w:
                ag_send(m, 0, 1, 2)
    one(1).start()

    places = lax.broadcasted_iota(jnp.int32, (SEQ, SEQ), 0)
    lanes = lax.broadcasted_iota(jnp.int32, (SEQ, SEQ), 1)
    key_seg = jnp.broadcast_to(seg[pl.ds(c, 1), :].astype(F32), (SEQ, SEQ))
    query_seg = key_seg.T
    allowed = (key_seg == query_seg) & (lanes <= places)
    earlier = jnp.sum(jnp.where(key_seg < query_seg, 1.0, 0.0), axis=1, keepdims=True)
    pos = places.astype(F32) - earlier
    angle = pos * freq[...]
    first_half = lax.rem(lanes, HEAD) < HEAD // 2
    cosr[...] = jnp.cos(angle)
    sinr[...] = jnp.where(first_half, -jnp.sin(angle), jnp.sin(angle))

    def swap(u):
        return jnp.where(first_half, pltpu.roll(u, 96, 1), pltpu.roll(u, 32, 1))

    ag_step(0)
    for copy in fetch[4:]:
        copy.wait()
    for k in range(2):
        src, _, dev = single[k]
        remote(src, (raw, draw)[k].at[sib_half], mi_s.at[k], mi_r.at[k], dev).wait_recv()

    @pl.when(sec == 0)
    def _():
        xin[...] = nn(raw[...], perm[...]).astype(BF)

    @pl.when(sec == 1)
    def _():
        din[...] = nn(draw[...], perm[...]).astype(BF)

    def ag_first(*ts):
        @pl.when(sec == 0)
        def _():
            for t in ts:
                ag_step(t)

    @pl.when(sec == 1)
    def _():
        for t in range(1, ag_steps):
            ag_step(t)
        ag_drain()
        for k in range(2, 6):
            one(k).wait_recv()

    ag_first(1, 2, 3, 4, 5, 6)

    def norm(v):
        inverse = lax.rsqrt(jnp.sum(v * v, axis=1, keepdims=True) * (1.0 / D) + EPS)
        return v * inverse, inverse

    def norm_back(d, normal, inverse):
        return inverse * (d - normal * (jnp.sum(normal * d, axis=1, keepdims=True) * (1.0 / D)))

    gains[...] = wq[:, 1536:1664].astype(F32).T[64:72, :]
    xhat, _ = norm(xin[...].astype(F32))
    xn1[...] = (xhat * gains[0:1, :]).astype(BF)
    qkv[...] = nn(xn1[...], wq[...])
    for t in range(QK // 128):
        cols = pl.ds(128 * t, 128)
        u = qkv[:, cols]
        qk[:, cols] = (u * cosr[...] + swap(u) * sinr[...]).astype(BF)
    vv[...] = qkv[:, QK:QKVP].astype(BF)
    ag_first(7)
    group = HEADS // KV_HEADS

    def head(hd):
        return slice(HEAD * hd, HEAD * (hd + 1))

    def key_of(hd):
        return qk[:, head(HEADS + hd // group)]

    def value_of(hd):
        return vv[:, head(hd // group)]

    scale = HEAD ** -0.5
    for hd in range(HEADS):
        pf[hd] = nt(qk[:, head(hd)], key_of(hd))
    for hd in range(HEADS):
        s = jnp.where(allowed, pf[hd] * scale, -1e30)
        e = jnp.exp(s - jnp.max(s, axis=1, keepdims=True))
        pf[hd] = e / jnp.sum(e, axis=1, keepdims=True)
    ag_first(8)
    o[:, HEADS * HEAD:] = jnp.zeros((SEQ, DP - HEADS * HEAD), BF)
    for hd in range(HEADS):
        o[:, head(hd)] = nn(pf[hd].astype(BF), value_of(hd)).astype(BF)
    h[...] = xin[...].astype(F32) + nt(o[...], wo[...])
    xhat, _ = norm(h[...])
    xn2[...] = (xhat * gains[1:2, :]).astype(BF)
    ag_first(9)

    def gated(j):
        cols = pl.ds(PART * j, PART)
        gate[:, cols] = nn(xn2[...], wg[:, cols])
        up[:, cols] = nn(xn2[...], wg[:, pl.ds(FF + PART * j, PART)])
        g_ = gate[:, cols]
        mm[:, cols] = (g_ * jax.nn.sigmoid(g_) * up[:, cols]).astype(BF)

    gated(0)
    ag_first(10, 11)
    gated(1)
    ag_first(12)
    dh[...] = h[...] + nt(mm[:, 0:PART], wd[:, 0:PART])
    ag_first(13)
    for k, cols in enumerate(own_cols):
        act[:, cols] = (dh[:, cols] + nt(mm[:, PART:], wd[cols, PART:])).astype(BF)

        @pl.when(sec == 0)
        def _():
            one(2 + k).start()

    @pl.when(sec == 0)
    def _():
        ag_drain()
        for k in range(2, 6):
            one(k).wait_send()
        one(6).wait_recv()

    pairs = ((xn1, dqkv), (da, o), (xn2, dgu), (din, mm))
    lower = pl.multiple_of(c * HALF, HALF)
    upper = pl.multiple_of((1 - c) * HALF, HALF)
    rs_table = (
        (upper, HALF, sibling), (mine[2, 0], 64, last_up), (mine[2, 1], 64, last_down), (mine[1, 1], 64, last_up),
        (mine[3, 0], 64, last_down), (mine[1, 0], 64, last_up), (mine[3, 1], 64, last_down), (mine[0, 1], 64, over_x),
        (slab[1], 16, first_to[0]), (slab[3], 16, first_to[1]), (slab[2], 16, first_to[2]), None,
    ) + tuple((row(cc, other_x, mod4(a + step)), 16, across[step]) for step in steps4)

    def rs_copy(m, k):
        w, first, cols = SUMS[m]
        sems = rs_s.at[m * N_RS + k], rs_r.at[m * N_RS + k]
        if k == 11:
            piece = fin[m].at[own16]
            return remote(piece, piece, *sems, sibling)
        start, rows, dev = rs_table[k]
        if m == ns - 1 and k in (1, 2):
            dev = last_far
        if k == 0:
            dst = rb[m]
        elif k < 7:
            dst = ra[m].at[pl.ds(64 * (k - 1), rows)]
        elif k == 7:
            dst = rx[m]
        elif k > 11:
            dst = rx[m].at[pl.ds(16 * (k - 12), 16)]
        else:
            dst = r3[m].at[pl.ds(16 * (k - 8), 16)]
        return remote(weights[w].at[pl.ds(start, rows), pl.ds(first, cols)], dst, *sems, dev)

    def rs_send(m, *ks):
        for k in ks:
            rs_copy(m, k).start()

    def rs_wait(m, *ks):
        for k in ks:
            rs_copy(m, k).wait_recv()

    def add_in(m, start, rows, source, source_row):
        w, first, cols = SUMS[m]
        ref = weights[w]
        width = 640 if cols % 640 == 0 else 512

        def body(tile):
            there = pl.ds(pl.multiple_of(tile.start + first, 128), tile.size)
            ref[pl.ds(start, rows), there] = ref[pl.ds(start, rows), there] + source[pl.ds(source_row, rows), tile]

        over(cols, width, body)

    def rs0(m):
        w, first, cols = SUMS[m]
        left, right = pairs[w]
        if first == 0:
            lts[w][...] = left[...].T

        def body(tile):
            there = pl.ds(pl.multiple_of(tile.start + first, 128), tile.size)
            for r in range(4):
                rows = pl.ds(256 * r, 256)
                weights[w][rows, there] = nn(lts[w][rows, :], right[:, there]).astype(BF)

        over(cols, 256, body)
        rs_send(m, 0)

    def rs1(m):
        rs_wait(m, 0)
        add_in(m, lower, HALF, rb[m], 0)
        rs_send(m, 1, 2, 3, 4)
        if m == ns - 1:
            rs_send(m, 5, 6)

    def rs2(m):
        if m == ns - 1:
            return
        for k, into in ((1, mine[1, 0]), (2, mine[3, 1])):
            rs_wait(m, k)
            add_in(m, into, 64, ra[m], 64 * (k - 1))
            rs_send(m, k + 4)

    def rs3(m):
        for k, s in ((3, 1), (4, 0), (5, 0), (6, 1)):
            rs_wait(m, k)
            add_in(m, mine[0, s], 64, ra[m], 64 * (k - 1))
        if m == ns - 1:
            for k in (1, 2):
                rs_wait(m, k)
                add_in(m, mine[0, k - 1], 64, ra[m], 64 * (k - 1))
            rs_send(m, 12, 13, 14, 15, 8, 9, 10)
        else:
            rs_send(m, 7)

    def rs4(m):
        if m == ns - 1:
            return
        rs_wait(m, 7)
        add_in(m, mine[0, 0], 64, rx[m], 0)
        rs_send(m, 8, 9, 10)

    def rs5(m):
        w, first, cols = SUMS[m]
        rs_wait(m, 8, 9, 10)
        total = weights[w][pl.ds(slab[0], 16), pl.ds(first, cols)].astype(F32)
        for k in range(3):
            total = total + r3[m][pl.ds(16 * k, 16), :].astype(F32)
        if m == ns - 1:
            rs_wait(m, 12, 13, 14, 15)
            for k in steps4:
                total = total + rx[m][pl.ds(16 * k, 16), :].astype(F32)
        fin[m][own16, :] = total
        rs_send(m, 11)

    def rs6(m):
        remote(fin[m].at[own16], fin[m].at[pl.ds(pl.multiple_of(16 * (1 - c), 16), 16)],
               rs_s.at[m * N_RS + 11], rs_r.at[m * N_RS + 11], sibling).wait_recv()
        for k in range(12) if m < ns - 1 else (*range(7), *range(8, 16)):
            rs_copy(m, k).wait_send()

    rs_order = ((rs0, 0), (rs1, 1), (rs2, 2), (rs3, 3), (rs4, 5), (rs5, 7), (rs6, 9))
    rs_steps = ns + 9

    def reduce(*ts):
        for t in ts:
            for stage, late in rs_order:
                if 0 <= t - late < ns and not (late < 2 and t - late < 2):
                    stage(t - late)

    def reduce_start():
        rs0(0)
        rs0(1)

    def reduce_links():
        rs1(0)
        rs1(1)

    def reduce_first(*ts):
        @pl.when(sec == 0)
        def _():
            reduce(*ts)

    for j in range(2):
        cols = pl.ds(PART * j, PART)
        dm = nn(din[...], wd[:, cols])
        g_ = gate[:, cols]
        sg = jax.nn.sigmoid(g_)
        dgu[:, cols] = (dm * up[:, cols] * sg * (1.0 + g_ * (1.0 - sg))).astype(BF)
        dgu[:, pl.ds(FF + PART * j, PART)] = (dm * g_ * sg).astype(BF)
    pl.when(sec == 0)(reduce_start)
    for cols in own_cols[:2]:
        dh[:, cols] = nt(dgu[...], wg[cols, :])
    pl.when(sec == 0)(reduce_links)
    for cols in own_cols[2:]:
        dh[:, cols] = nt(dgu[...], wg[cols, :])
    reduce_first(2)
    xhat, inv = norm(h[...])
    dhv = din[...].astype(F32) + norm_back(dh[...] * gains[1:2, :], xhat, inv)
    dh[...] = dhv
    da[...] = dhv.astype(BF)
    do[...] = nn(da[...], wo[...]).astype(BF)
    reduce_first(3)
    for hd in range(HEADS):
        dps[hd] = nt(do[:, head(hd)], value_of(hd))
    for hd in range(HEADS):
        p, dp = pf[hd], dps[hd]
        dsb[hd] = (p * (dp - jnp.sum(dp * p, axis=1, keepdims=True))).astype(BF)
    reduce_first(4)
    dqkv[:, QKV:] = jnp.zeros((SEQ, QKVP - QKV), BF)
    for hd in range(HEADS):
        dqkf[:, head(hd)] = nn(dsb[hd], key_of(hd)) * scale
    for g in range(KV_HEADS):
        hds = range(group * g, group * (g + 1))
        dqkf[:, head(HEADS + g)] = sum(tn(dsb[hd], qk[:, head(hd)]) for hd in hds) * scale
        dv = sum(tn(pf[hd].astype(BF), do[:, head(hd)]) for hd in hds)
        dqkv[:, QK + HEAD * g:QK + HEAD * (g + 1)] = dv.astype(BF)
    reduce_first(5)
    for t in range(QK // 128):
        cols = pl.ds(128 * t, 128)
        u = dqkf[:, cols]
        dqkv[:, cols] = (u * cosr[...] - swap(u) * sinr[...]).astype(BF)
    h[...] = nt(dqkv[...], wq[...])
    reduce_first(6)
    xhat, inv = norm(xin[...].astype(F32))
    ig[...] = (dh[...] + norm_back(h[...] * gains[0:1, :], xhat, inv)).astype(BF)

    @pl.when(sec == 1)
    def _():
        one(6).start()
        reduce_start()
        reduce_links()
        reduce(2, 3, 4, 5, 6)

    reduce(7, 8, 9)
    a960[...] = nt(act[...], perm[...]).astype(BF)
    acts[c] = a960[own_half, :]
    one(7).start()
    i960[...] = nt(ig[...], perm[...]).astype(BF)
    igrad[c] = i960[own_half, :]
    one(8).start()
    reduce(10, 11, 12)
    for k in (7, 8):
        src, dst, dev = single[k]
        remote(src, (acts, igrad)[k - 7].at[1 - c], mi_s.at[k], mi_r.at[k], dev).wait_recv()
        one(k).wait_send()

    @pl.when(sec == 1)
    def _():
        one(6).wait_send()

    one(0).wait_send()
    one(1).wait_send()
    reduce(*range(13, rs_steps - 2))

    sums = [0.0] * 4
    for m, (w, first, cols) in enumerate(SUMS):
        if w in (0, 2):
            cols = min(cols, (QKV, D, 2 * FF, FF)[w])
            shard = (pq, po, pg, pd)[w][:, first:first + cols].astype(F32)
            sums[w] = sums[w] + jnp.sum(fin[m][:, 0:cols] * shard, axis=1, keepdims=True)
    gga[...] = jnp.broadcast_to(sums[0], (32, 128)).T[0:1, 0:ROWS] / ga[...].astype(F32)
    ggf[...] = jnp.broadcast_to(sums[2], (32, 128)).T[0:1, 0:ROWS] / gf[...].astype(F32)
    reduce(rs_steps - 2, rs_steps - 1)


def lay_out(*refs):
    n = len(SUMS)
    passed, fin, rest = refs[:4], refs[4:4 + n], refs[4 + n:]
    acts, igrad, gga, ggf, gq, go, gg, gd = rest
    for source, target in zip(passed, (acts, igrad, gga, ggf)):
        target[...] = source[...]
    targets = (gq, go, gg, gd)
    for m, (w, first, cols) in enumerate(SUMS):
        cols = min(cols, (QKV, D, 2 * FF, FF)[w])
        targets[w][:, 0, first:first + cols] = fin[m][0:ROWS, 0:cols]


def per_device(tokens, segments, gain_attn, w_qkv, w_out, gain_ffn, w_gu, w_down, d_out):
    n, ns = len(PIECES), len(SUMS)
    vmem = pl.BlockSpec(memory_space=pltpu.VMEM)
    per_sum = lambda rows: [pltpu.VMEM((rows, cols), BF) for _, _, cols in SUMS]
    scratch = (
        [pltpu.VMEM((DP, w), BF) for w in WIDTHS]
        + [pltpu.VMEM((ROWS, w), BF) for w in (QKV, D, 2 * FF, FF)]
        + [pltpu.VMEM((32, w), BF) for w in WIDTHS]
        + per_sum(HALF) + per_sum(384) + per_sum(64) + per_sum(48)
        + [pltpu.VMEM((DP, SEQ), BF)] * 4
        + [
            pltpu.VMEM((D, DP), BF),
            pltpu.VMEM((SEQ, D), BF), pltpu.VMEM((SEQ, D), BF),
            pltpu.VMEM((SEQ, DP), BF), pltpu.VMEM((SEQ, DP), BF),
            pltpu.VMEM((SEQ, DP), BF), pltpu.VMEM((SEQ, DP), BF),
            pltpu.VMEM((SEQ, D), BF), pltpu.VMEM((SEQ, D), BF),
            pltpu.VMEM((SEQ, QKVP), F32), pltpu.VMEM((SEQ, QK), BF), pltpu.VMEM((SEQ, QKVP - QK), BF),
            pltpu.VMEM((HEADS, SEQ, SEQ), F32), pltpu.VMEM((SEQ, DP), BF), pltpu.VMEM((SEQ, DP), F32),
            pltpu.VMEM((SEQ, DP), BF), pltpu.VMEM((SEQ, DP), BF),
            pltpu.VMEM((SEQ, FF), F32), pltpu.VMEM((SEQ, FF), F32), pltpu.VMEM((SEQ, FF), BF),
            pltpu.VMEM((SEQ, 2 * FF), BF), pltpu.VMEM((SEQ, DP), F32),
            pltpu.VMEM((SEQ, DP), BF), pltpu.VMEM((SEQ, DP), BF),
            pltpu.VMEM((HEADS, SEQ, SEQ), F32), pltpu.VMEM((HEADS, SEQ, SEQ), BF),
            pltpu.VMEM((SEQ, QK), F32), pltpu.VMEM((SEQ, QKVP), BF),
            pltpu.VMEM((SEQ, SEQ), F32), pltpu.VMEM((SEQ, SEQ), F32), pltpu.VMEM((8, DP), F32),
        ]
        + [pltpu.SemaphoreType.DMA((7,))]
        + [pltpu.SemaphoreType.DMA((n * N_AG,))] * 2
        + [pltpu.SemaphoreType.DMA((ns * N_RS,))] * 2
        + [pltpu.SemaphoreType.DMA((9,))] * 2
    )
    shape = jax.ShapeDtypeStruct
    hbm = pl.BlockSpec(memory_space=pl.ANY)
    passed = (shape(tokens.shape, BF), shape(tokens.shape, BF), shape((1, ROWS), F32), shape((1, ROWS), F32))
    out = pl.pallas_call(
        kernel,
        out_shape=passed + tuple(shape((32, cols), F32) for _, _, cols in SUMS),
        in_specs=[hbm, vmem, vmem, hbm, hbm, vmem, hbm, hbm, hbm, hbm, vmem],
        out_specs=(vmem,) * (4 + ns),
        scratch_shapes=scratch,
        compiler_params=pltpu.CompilerParams(
            collective_id=0, has_side_effects=True, vmem_limit_bytes=63 * 1024 * 1024
        ),
    )(
        tokens, segments, gain_attn, w_qkv[0], w_out[0], gain_ffn, w_gu[0], w_down[0], d_out,
        jnp.asarray(permutation(), BF), jnp.asarray(lane_frequencies(), F32),
    )
    acts, igrad, gga, ggf, gq, go, gg, gd = pl.pallas_call(
        lay_out,
        out_shape=passed + tuple(shape((ROWS, 1, cols), F32) for cols in (QKV, D, 2 * FF, FF)),
        in_specs=[vmem] * (4 + ns),
        out_specs=(vmem,) * 8,
    )(*out)
    gq, go, gg, gd = (jnp.swapaxes(g, 0, 1) for g in (gq, go, gg, gd))
    return acts[None], igrad[None], gga, gq, go, ggf, gg, gd


def solution(mesh):
    in_specs = (
        P(None, ("fsdp", "ctx"), None),
        P(None, "fsdp"),
        P("section", "fsdp"),
        P("section", "fsdp", None),
        P("section", "fsdp", None),
        P("section", "fsdp"),
        P("section", "fsdp", None),
        P("section", "fsdp", None),
        P(None, ("fsdp", "ctx"), None),
    )
    out_specs = (
        P("section", None, ("fsdp", "ctx"), None),
        P("section", None, ("fsdp", "ctx"), None),
        P("section", "fsdp"),
        P("section", "fsdp", None),
        P("section", "fsdp", None),
        P("section", "fsdp"),
        P("section", "fsdp", None),
        P("section", "fsdp", None),
    )
    return jax.shard_map(
        per_device, mesh=mesh, in_specs=in_specs, out_specs=out_specs, check_vma=False
    )
```

```python
import functools

import jax
import jax.numpy as jnp
import numpy as np
from jax import lax
from jax.experimental import pallas as pl
from jax.experimental.pallas import tpu as pltpu
from jax.sharding import PartitionSpec as P

D = 960
HEADS = 15
KV_HEADS = 5
HEAD = 64
FF = 2560
SEQ = 128
EPS = 1e-05
BASE = 100000.0

DP = 1024
HALF = DP // 2
QKV = 1600
QKVP = 1664
QK = 1280
ROWS = 30
BF = jnp.bfloat16
F32 = jnp.float32
MESH = pl.DeviceIdType.MESH

PART = FF // 2
PIECES = (
    (0, 0, QKVP, 1), (1, 0, DP, 0), (2, 0, PART, 0), (2, FF, PART, 1), (2, PART, PART, 0), (2, FF + PART, PART, 1),
    (3, 0, PART, 0), (3, PART, PART, 0),
)
SUMS = (
    (3, 0, 640), (3, 640, 640), (2, 0, PART), (2, FF, PART), (2, PART, PART), (2, FF + PART, PART), (1, 0, DP), (0, 0, QKVP),
    (3, PART, 640), (3, PART + 640, 640),
)
WIDTHS = (QKVP, DP, 2 * FF, FF)
N_AG = 19
N_RS = 16


def permutation():
    table = np.zeros((D, DP), np.float32)
    for d in range(D):
        f, r = divmod(d, ROWS)
        y, z, x = f // 8, (f // 2) % 4, f % 2
        h, rr = divmod(r, 16)
        at = (z * 2 + x) * 4 + y if h == 0 else (y * 2 + x) * 4 + z
        table[d, h * HALF + at * 16 + rr] = 1.0
    return table


def lane_frequencies():
    i = np.arange(128) % 32
    return np.power(np.float32(BASE), -(i.astype(np.float32)) * np.float32(2.0 / HEAD))[None, :].astype(np.float32)


def nn(a, b):
    return lax.dot_general(a, b, (((1,), (0,)), ((), ())), preferred_element_type=F32)


def nt(a, b):
    return lax.dot_general(a, b, (((1,), (1,)), ((), ())), preferred_element_type=F32)


def tn(a, b):
    return lax.dot_general(a, b, (((0,), (0,)), ((), ())), preferred_element_type=F32)


def over(total, tile, body):
    whole = total // tile

    @pl.loop(0, whole)
    def _(i):
        body(pl.ds(pl.multiple_of(i * tile, tile), tile))

    if total % tile:
        body(pl.ds(whole * tile, total % tile))


def kernel(
    tok, seg, ga, wq_in, wo_in, gf, wg_in, wd_in, dout, perm_in, freq,
    acts, igrad, gga, ggf, *rest,
):
    n = len(PIECES)
    ns = len(SUMS)
    fin, rest = rest[:ns], rest[ns:]
    (wq, wo, wg, wd), rest = rest[:4], rest[4:]
    shards, rest = rest[:4], rest[4:]
    (pq, po, pg, pd), rest = rest[:4], rest[4:]
    rb, ra, rx, r3 = (rest[k * ns:(k + 1) * ns] for k in range(4))
    rest = rest[4 * ns:]
    lts, rest = rest[:4], rest[4:]
    (
        perm, raw, draw, xin, din, act, ig, a960, i960,
        qkv, qk, vv, pf, o, h, xn1, xn2, gate, up, mm,
        dgu, dh, da, do, dps, dsb, dqkf, dqkv, cosr, sinr, gains,
        in_s, ag_s, ag_r, rs_s, rs_r, mi_s, mi_r,
    ) = rest
    weights = (wq, wo, wg, wd)

    sec = lax.axis_index("section")
    f = lax.axis_index("fsdp")
    c = lax.axis_index("ctx")
    y = f // 8
    z = lax.rem(f // 2, 4)
    x = lax.rem(f, 2)
    a = y + c * (z - y)
    cc = z + c * (y - z)
    other_x = 1 - x

    def at(a_, x_, cc_):
        yy = a_ + c * (cc_ - a_)
        zz = cc_ + c * (a_ - cc_)
        return (sec, (yy * 4 + zz) * 2 + x_, c)

    def mod4(v):
        return lax.rem(v + 4, 4)

    def row(cc_, x_, a_, half=None):
        half = c if half is None else half
        return pl.multiple_of(half * HALF + ((cc_ * 2 + x_) * 4 + a_) * 16, 16)

    own_half = pl.ds(pl.multiple_of(64 * c, 64), 64)
    sib_half = pl.ds(pl.multiple_of(64 * (1 - c), 64), 64)
    own16 = pl.ds(pl.multiple_of(16 * c, 16), 16)
    fetch = [
        pltpu.make_async_copy(src, dst, in_s.at[k])
        for k, (src, dst) in enumerate((
            (wq_in, shards[0]), (wo_in, shards[1]), (wg_in, shards[2]), (wd_in, shards[3]),
            (tok.at[c], raw.at[own_half]), (dout.at[c], draw.at[own_half]), (perm_in, perm),
        ))
    ]
    for copy in fetch:
        copy.start()

    sibling = (sec, f, 1 - c)
    partner = (1 - sec, f, c)
    last_up, last_down = at(a, x, mod4(cc + 1)), at(a, x, mod4(cc + 3))
    over_x = at(a, other_x, cc)
    first_to = [at(mod4(a + step), x, cc) for step in (1, 3, 2)]
    last_far = at(a, x, mod4(cc + 2))
    across = [at(mod4(a + step), other_x, cc) for step in range(4)]

    barrier = pltpu.get_barrier_semaphore()
    friends = first_to + across + [last_up, last_down, last_far, sibling, partner]
    for dev in friends:
        pl.semaphore_signal(barrier, inc=1, device_id=dev, device_id_type=MESH)

    gains[...] = jnp.zeros_like(gains)
    gains[0:1, 0:ROWS] = ga[...].astype(F32)
    gains[1:2, 0:ROWS] = gf[...].astype(F32)
    gain_cols = gains[0:8, 0:128].T
    pl.semaphore_wait(barrier, len(friends))

    def remote(src, dst, ssem, rsem, dev):
        return pltpu.make_async_remote_copy(
            src_ref=src, dst_ref=dst, send_sem=ssem, recv_sem=rsem, device_id=dev, device_id_type=MESH
        )

    own_cols = [pl.ds(256 * k, 256) for k in range(4)]
    single = (
        [(tok.at[1 - c], raw.at[own_half], sibling), (dout.at[1 - c], draw.at[own_half], sibling)]
        + [(act.at[:, cols], xin.at[:, cols], partner) for cols in own_cols]
        + [(ig, din, partner), (a960.at[sib_half], acts.at[c], sibling), (i960.at[sib_half], igrad.at[c], sibling)]
    )

    def one(k):
        src, dst, dev = single[k]
        return remote(src, dst, mi_s.at[k], mi_r.at[k], dev)

    steps4 = range(4)
    xs = (x, other_x)
    mine = {(d, s): row(mod4(cc + d), xs[s], 0) for d in steps4 for s in range(2)}
    theirs = {(d, s): row(mod4(a + d), xs[s], 0, 1 - c) for d in steps4 for s in range(2)}
    slab = [row(cc, x, mod4(a + d)) for d in steps4]
    ag_table = [
        (slab[0], slab[3], 16, first_to[0]),
        (slab[0], slab[1], 16, first_to[1]),
        (slab[0], slab[2], 16, first_to[2]),
        (mine[0, 0], mine[0, 1], 64, over_x),
        (mine[0, 0], mine[3, 0], 64, last_up),
        (mine[0, 0], mine[1, 0], 64, last_down),
        (mine[0, 1], mine[3, 1], 64, last_up),
        (mine[0, 1], mine[1, 1], 64, last_down),
        (mine[3, 0], mine[2, 0], 64, last_up),
        (mine[1, 1], mine[2, 1], 64, last_down),
    ] + [
        (mine[key], theirs[key], 64, sibling)
        for key in ((0, 0), (0, 1), (3, 0), (1, 0), (3, 1), (1, 1), (2, 0), (2, 1))
    ]

    ag_table.append((mine[2, 0], mine[2, 1], 64, over_x))
    ag_parts = {
        8: (pl.multiple_of(mine[3, 0], 32), pl.multiple_of(mine[2, 0], 32), 32, last_up),
        9: (pl.multiple_of(mine[1, 0] + 32, 32), pl.multiple_of(mine[2, 0] + 32, 32), 32, last_down),
    }

    def ag_copy(m, k, arriving=False):
        w, first, cols, wide = PIECES[m]
        source, landing, rows, dev = ag_parts[k] if wide and k in ag_parts else ag_table[k]
        piece = weights[w].at[pl.ds(landing if arriving else source, rows), pl.ds(first, cols)]
        return remote(piece, piece, ag_s.at[m * N_AG + k], ag_r.at[m * N_AG + k], dev)

    def ag_send(m, *ks):
        for k in ks:
            ag_copy(m, k).start()

    def ag_wait(m, *ks):
        for k in ks:
            ag_copy(m, k, True).wait_recv()

    def ag1(m):
        ag_wait(m, 0, 1, 2)
        ag_send(m, 4, 5, 3, 10)

    def ag2(m):
        ag_wait(m, 3)
        ag_send(m, 6, 7, 11)
        ag_wait(m, 4)
        ag_send(m, 8, 12)
        ag_wait(m, 5)
        if PIECES[m][3]:
            ag_send(m, 9)
        ag_send(m, 13)

    def ag3(m):
        ag_wait(m, 7)
        if not PIECES[m][3]:
            ag_send(m, 9)
        ag_send(m, 15)
        ag_wait(m, 6)
        ag_send(m, 14)

    def ag4(m):
        if PIECES[m][3]:
            ag_wait(m, 8, 9)
            ag_send(m, 18, 16)
        else:
            ag_wait(m, 8)
            ag_send(m, 16)
            ag_wait(m, 9)
            ag_send(m, 17)

    def ag5(m):
        if PIECES[m][3]:
            ag_wait(m, 18)
            ag_send(m, 17)

    def ag6(m):
        ag_wait(m, *range(10, 18))

    ag_steps = n + 6

    def ag_step(t):
        for stage, late in ((ag1, 0), (ag2, 2), (ag3, 3), (ag4, 4), (ag5, 5), (ag6, 6)):
            if 0 <= t - late < n:
                stage(t - late)

    def ag_drain():
        for m in range(n):
            for k in range(N_AG if PIECES[m][3] else N_AG - 1):
                ag_copy(m, k).wait_send()

    one(0).start()
    for w, (pack, cols) in enumerate(((pq, QKV), (po, D), (pg, 2 * FF), (pd, FF))):
        if cols < pack.shape[1]:
            pack[:, cols:] = jnp.zeros((32, pack.shape[1] - cols), BF)
        pack[16:32, :] = jnp.zeros((16, pack.shape[1]), BF)
        fetch[w].wait()
        pack[0:ROWS, 0:cols] = shards[w][...]
        if w == 0:
            pack[:, QKV:QKV + 2] = gain_cols[0:32, 0:2].astype(BF)
        weights[w][pl.ds(slab[0], 16), :] = pack[own16, :]
        for m in range(n):
            if PIECES[m][0] == w:
                ag_send(m, 0, 1, 2)
    one(1).start()

    places = lax.broadcasted_iota(jnp.int32, (SEQ, SEQ), 0)
    lanes = lax.broadcasted_iota(jnp.int32, (SEQ, SEQ), 1)
    key_seg = jnp.broadcast_to(seg[pl.ds(c, 1), :].astype(F32), (SEQ, SEQ))
    query_seg = key_seg.T
    allowed = (key_seg == query_seg) & (lanes <= places)
    earlier = jnp.sum(jnp.where(key_seg < query_seg, 1.0, 0.0), axis=1, keepdims=True)
    pos = places.astype(F32) - earlier
    angle = pos * freq[...]
    first_half = lax.rem(lanes, HEAD) < HEAD // 2
    cosr[...] = jnp.cos(angle)
    sinr[...] = jnp.where(first_half, -jnp.sin(angle), jnp.sin(angle))

    def swap(u):
        return jnp.where(first_half, pltpu.roll(u, 96, 1), pltpu.roll(u, 32, 1))

    ag_step(0)
    for copy in fetch[4:]:
        copy.wait()
    for k in range(2):
        src, _, dev = single[k]
        remote(src, (raw, draw)[k].at[sib_half], mi_s.at[k], mi_r.at[k], dev).wait_recv()

    @pl.when(sec == 0)
    def _():
        xin[...] = nn(raw[...], perm[...]).astype(BF)

    @pl.when(sec == 1)
    def _():
        din[...] = nn(draw[...], perm[...]).astype(BF)

    def read_gains():
        gains[...] = wq[:, 1536:1664].astype(F32).T[64:72, :]

    def ag_first(*ts):
        @pl.when(sec == 0)
        def _():
            for t in ts:
                ag_step(t)

    @pl.when(sec == 1)
    def _():
        for t in range(1, ag_steps):
            ag_step(t)
        ag_drain()
        read_gains()
        for k in range(2, 6):
            one(k).wait_recv()

    ag_first(1, 2, 3, 4, 5, 6)
    pl.when(sec == 0)(read_gains)

    def norm(v):
        inverse = lax.rsqrt(jnp.sum(v * v, axis=1, keepdims=True) * (1.0 / D) + EPS)
        return v * inverse, inverse

    def norm_back(d, normal, inverse):
        return inverse * (d - normal * (jnp.sum(normal * d, axis=1, keepdims=True) * (1.0 / D)))

    xhat, _ = norm(xin[...].astype(F32))
    xn1[...] = (xhat * gains[0:1, :]).astype(BF)
    qkv[...] = nn(xn1[...], wq[...])
    for t in range(QK // 128):
        cols = pl.ds(128 * t, 128)
        u = qkv[:, cols]
        qk[:, cols] = (u * cosr[...] + swap(u) * sinr[...]).astype(BF)
    vv[...] = qkv[:, QK:QKVP].astype(BF)
    ag_first(7)
    group = HEADS // KV_HEADS

    def head(hd):
        return slice(HEAD * hd, HEAD * (hd + 1))

    def key_of(hd):
        return qk[:, head(HEADS + hd // group)]

    def value_of(hd):
        return vv[:, head(hd // group)]

    scale = HEAD ** -0.5
    for hd in range(HEADS):
        pf[hd] = nt(qk[:, head(hd)], key_of(hd))
    for hd in range(HEADS):
        s = jnp.where(allowed, pf[hd] * scale, -1e30)
        e = jnp.exp(s - jnp.max(s, axis=1, keepdims=True))
        pf[hd] = e / jnp.sum(e, axis=1, keepdims=True)
    ag_first(8)
    o[:, HEADS * HEAD:] = jnp.zeros((SEQ, DP - HEADS * HEAD), BF)
    for hd in range(HEADS):
        o[:, head(hd)] = nn(pf[hd].astype(BF), value_of(hd)).astype(BF)
    h[...] = xin[...].astype(F32) + nt(o[...], wo[...])
    xhat, _ = norm(h[...])
    xn2[...] = (xhat * gains[1:2, :]).astype(BF)
    ag_first(9)

    def gated(j):
        cols = pl.ds(PART * j, PART)
        gate[:, cols] = nn(xn2[...], wg[:, cols])
        up[:, cols] = nn(xn2[...], wg[:, pl.ds(FF + PART * j, PART)])
        g_ = gate[:, cols]
        mm[:, cols] = (g_ * jax.nn.sigmoid(g_) * up[:, cols]).astype(BF)

    gated(0)
    ag_first(10, 11)
    gated(1)
    ag_first(12)
    dh[...] = h[...] + nt(mm[:, 0:PART], wd[:, 0:PART])
    ag_first(13)
    for k, cols in enumerate(own_cols):
        act[:, cols] = (dh[:, cols] + nt(mm[:, PART:], wd[cols, PART:])).astype(BF)

        @pl.when(sec == 0)
        def _():
            one(2 + k).start()

    @pl.when(sec == 0)
    def _():
        ag_drain()
        for k in range(2, 6):
            one(k).wait_send()
        one(6).wait_recv()

    pairs = ((xn1, dqkv), (da, o), (xn2, dgu), (din, mm))
    lower = pl.multiple_of(c * HALF, HALF)
    upper = pl.multiple_of((1 - c) * HALF, HALF)
    rs_table = (
        (upper, HALF, sibling), (mine[2, 0], 64, last_up), (mine[2, 1], 64, last_down), (mine[1, 1], 64, last_up),
        (mine[3, 0], 64, last_down), (mine[1, 0], 64, last_up), (mine[3, 1], 64, last_down), (mine[0, 1], 64, over_x),
        (slab[1], 16, first_to[0]), (slab[3], 16, first_to[1]), (slab[2], 16, first_to[2]), None,
    ) + tuple((row(cc, other_x, mod4(a + step)), 16, across[step]) for step in steps4)

    def rs_copy(m, k):
        w, first, cols = SUMS[m]
        sems = rs_s.at[m * N_RS + k], rs_r.at[m * N_RS + k]
        if k == 11:
            piece = fin[m].at[own16]
            return remote(piece, piece, *sems, sibling)
        start, rows, dev = rs_table[k]
        if m == ns - 1 and k in (1, 2):
            dev = last_far
        if k == 0:
            dst = rb[m]
        elif k < 7:
            dst = ra[m].at[pl.ds(64 * (k - 1), rows)]
        elif k == 7:
            dst = rx[m]
        elif k > 11:
            dst = rx[m].at[pl.ds(16 * (k - 12), 16)]
        else:
            dst = r3[m].at[pl.ds(16 * (k - 8), 16)]
        return remote(weights[w].at[pl.ds(start, rows), pl.ds(first, cols)], dst, *sems, dev)

    def rs_send(m, *ks):
        for k in ks:
            rs_copy(m, k).start()

    def rs_wait(m, *ks):
        for k in ks:
            rs_copy(m, k).wait_recv()

    def add_in(m, start, rows, source, source_row):
        w, first, cols = SUMS[m]
        ref = weights[w]
        width = 640 if cols % 640 == 0 else 512

        def body(tile):
            there = pl.ds(pl.multiple_of(tile.start + first, 128), tile.size)
            ref[pl.ds(start, rows), there] = ref[pl.ds(start, rows), there] + source[pl.ds(source_row, rows), tile]

        over(cols, width, body)

    def rs0(m):
        w, first, cols = SUMS[m]
        left, right = pairs[w]
        if first == 0:
            lts[w][...] = left[...].T

        def body(tile):
            there = pl.ds(pl.multiple_of(tile.start + first, 128), tile.size)
            for r in range(4):
                rows = pl.ds(256 * r, 256)
                weights[w][rows, there] = nn(lts[w][rows, :], right[:, there]).astype(BF)

        over(cols, 256, body)
        rs_send(m, 0)

    def rs1(m):
        rs_wait(m, 0)
        add_in(m, lower, HALF, rb[m], 0)
        rs_send(m, 1, 2, 3, 4)
        if m == ns - 1:
            rs_send(m, 5, 6)

    def rs2(m):
        if m == ns - 1:
            return
        for k, into in ((1, mine[1, 0]), (2, mine[3, 1])):
            rs_wait(m, k)
            add_in(m, into, 64, ra[m], 64 * (k - 1))
            rs_send(m, k + 4)

    def rs3(m):
        for k, s in ((3, 1), (4, 0), (5, 0), (6, 1)):
            rs_wait(m, k)
            add_in(m, mine[0, s], 64, ra[m], 64 * (k - 1))
        if m == ns - 1:
            for k in (1, 2):
                rs_wait(m, k)
                add_in(m, mine[0, k - 1], 64, ra[m], 64 * (k - 1))
            rs_send(m, 12, 13, 14, 15, 8, 9, 10)
        else:
            rs_send(m, 7)

    def rs4(m):
        if m == ns - 1:
            return
        rs_wait(m, 7)
        add_in(m, mine[0, 0], 64, rx[m], 0)
        rs_send(m, 8, 9, 10)

    def rs5(m):
        w, first, cols = SUMS[m]
        rs_wait(m, 8, 9, 10)
        total = weights[w][pl.ds(slab[0], 16), pl.ds(first, cols)].astype(F32)
        for k in range(3):
            total = total + r3[m][pl.ds(16 * k, 16), :].astype(F32)
        if m == ns - 1:
            rs_wait(m, 12, 13, 14, 15)
            for k in steps4:
                total = total + rx[m][pl.ds(16 * k, 16), :].astype(F32)
        fin[m][own16, :] = total
        rs_send(m, 11)

    def rs6(m):
        remote(fin[m].at[own16], fin[m].at[pl.ds(pl.multiple_of(16 * (1 - c), 16), 16)],
               rs_s.at[m * N_RS + 11], rs_r.at[m * N_RS + 11], sibling).wait_recv()
        for k in range(12) if m < ns - 1 else (*range(7), *range(8, 16)):
            rs_copy(m, k).wait_send()

    rs_order = ((rs1, 1), (rs0, 0), (rs2, 2), (rs3, 3), (rs4, 5), (rs5, 7), (rs6, 9))
    rs_steps = ns + 9

    def reduce(*ts):
        for t in ts:
            for stage, late in rs_order:
                if 0 <= t - late < ns and not (late < 2 and t - late < 2):
                    stage(t - late)

    def reduce_start():
        rs0(0)
        rs0(1)

    def reduce_links():
        rs1(0)
        rs1(1)

    def reduce_first(*ts):
        @pl.when(sec == 0)
        def _():
            reduce(*ts)

    for j in range(2):
        cols = pl.ds(PART * j, PART)
        dm = nn(din[...], wd[:, cols])
        g_ = gate[:, cols]
        sg = jax.nn.sigmoid(g_)
        dgu[:, cols] = (dm * up[:, cols] * sg * (1.0 + g_ * (1.0 - sg))).astype(BF)
        dgu[:, pl.ds(FF + PART * j, PART)] = (dm * g_ * sg).astype(BF)
    pl.when(sec == 0)(reduce_start)
    for cols in own_cols[:2]:
        dh[:, cols] = nt(dgu[...], wg[cols, :])
    pl.when(sec == 0)(reduce_links)
    for cols in own_cols[2:]:
        dh[:, cols] = nt(dgu[...], wg[cols, :])
    reduce_first(2)
    xhat, inv = norm(h[...])
    dhv = din[...].astype(F32) + norm_back(dh[...] * gains[1:2, :], xhat, inv)
    dh[...] = dhv
    da[...] = dhv.astype(BF)
    do[...] = nn(da[...], wo[...]).astype(BF)
    reduce_first(3)
    for hd in range(HEADS):
        dps[hd] = nt(do[:, head(hd)], value_of(hd))
    for hd in range(HEADS):
        p, dp = pf[hd], dps[hd]
        dsb[hd] = (p * (dp - jnp.sum(dp * p, axis=1, keepdims=True))).astype(BF)
    reduce_first(4)
    dqkv[:, QKV:] = jnp.zeros((SEQ, QKVP - QKV), BF)
    for hd in range(HEADS):
        dqkf[:, head(hd)] = nn(dsb[hd], key_of(hd)) * scale
    for g in range(KV_HEADS):
        hds = range(group * g, group * (g + 1))
        dqkf[:, head(HEADS + g)] = sum(tn(dsb[hd], qk[:, head(hd)]) for hd in hds) * scale
        dv = sum(tn(pf[hd].astype(BF), do[:, head(hd)]) for hd in hds)
        dqkv[:, QK + HEAD * g:QK + HEAD * (g + 1)] = dv.astype(BF)
    reduce_first(5)
    for t in range(QK // 128):
        cols = pl.ds(128 * t, 128)
        u = dqkf[:, cols]
        dqkv[:, cols] = (u * cosr[...] - swap(u) * sinr[...]).astype(BF)
    h[...] = nt(dqkv[...], wq[...])
    reduce_first(6)
    xhat, inv = norm(xin[...].astype(F32))
    ig[...] = (dh[...] + norm_back(h[...] * gains[0:1, :], xhat, inv)).astype(BF)

    @pl.when(sec == 1)
    def _():
        one(6).start()
        reduce_start()
        reduce_links()
        reduce(2, 3, 4, 5, 6)

    reduce(7, 8, 9)
    a960[...] = nt(act[...], perm[...]).astype(BF)
    acts[c] = a960[own_half, :]
    one(7).start()
    i960[...] = nt(ig[...], perm[...]).astype(BF)
    igrad[c] = i960[own_half, :]
    one(8).start()
    reduce(10, 11, 12)
    for k in (7, 8):
        src, dst, dev = single[k]
        remote(src, (acts, igrad)[k - 7].at[1 - c], mi_s.at[k], mi_r.at[k], dev).wait_recv()
        one(k).wait_send()

    @pl.when(sec == 1)
    def _():
        one(6).wait_send()

    one(0).wait_send()
    one(1).wait_send()
    reduce(*range(13, rs_steps - 2))

    sums = [0.0] * 4
    for m, (w, first, cols) in enumerate(SUMS):
        if w in (0, 2):
            cols = min(cols, (QKV, D, 2 * FF, FF)[w])
            shard = (pq, po, pg, pd)[w][:, first:first + cols].astype(F32)
            sums[w] = sums[w] + jnp.sum(fin[m][:, 0:cols] * shard, axis=1, keepdims=True)
    gga[...] = jnp.broadcast_to(sums[0], (32, 128)).T[0:1, 0:ROWS] / ga[...].astype(F32)
    ggf[...] = jnp.broadcast_to(sums[2], (32, 128)).T[0:1, 0:ROWS] / gf[...].astype(F32)
    reduce(rs_steps - 2, rs_steps - 1)


def lay_out(*refs):
    n = len(SUMS)
    passed, fin, rest = refs[:4], refs[4:4 + n], refs[4 + n:]
    acts, igrad, gga, ggf, gq, go, gg, gd = rest
    for source, target in zip(passed, (acts, igrad, gga, ggf)):
        target[...] = source[...]
    targets = (gq, go, gg, gd)
    for m, (w, first, cols) in enumerate(SUMS):
        cols = min(cols, (QKV, D, 2 * FF, FF)[w])
        targets[w][:, 0, first:first + cols] = fin[m][0:ROWS, 0:cols]


def per_device(tokens, segments, gain_attn, w_qkv, w_out, gain_ffn, w_gu, w_down, d_out):
    n, ns = len(PIECES), len(SUMS)
    vmem = pl.BlockSpec(memory_space=pltpu.VMEM)
    per_sum = lambda rows: [pltpu.VMEM((rows, cols), BF) for _, _, cols in SUMS]
    scratch = (
        [pltpu.VMEM((DP, w), BF) for w in WIDTHS]
        + [pltpu.VMEM((ROWS, w), BF) for w in (QKV, D, 2 * FF, FF)]
        + [pltpu.VMEM((32, w), BF) for w in WIDTHS]
        + per_sum(HALF) + per_sum(384) + per_sum(64) + per_sum(48)
        + [pltpu.VMEM((DP, SEQ), BF)] * 4
        + [
            pltpu.VMEM((D, DP), BF),
            pltpu.VMEM((SEQ, D), BF), pltpu.VMEM((SEQ, D), BF),
            pltpu.VMEM((SEQ, DP), BF), pltpu.VMEM((SEQ, DP), BF),
            pltpu.VMEM((SEQ, DP), BF), pltpu.VMEM((SEQ, DP), BF),
            pltpu.VMEM((SEQ, D), BF), pltpu.VMEM((SEQ, D), BF),
            pltpu.VMEM((SEQ, QKVP), F32), pltpu.VMEM((SEQ, QK), BF), pltpu.VMEM((SEQ, QKVP - QK), BF),
            pltpu.VMEM((HEADS, SEQ, SEQ), F32), pltpu.VMEM((SEQ, DP), BF), pltpu.VMEM((SEQ, DP), F32),
            pltpu.VMEM((SEQ, DP), BF), pltpu.VMEM((SEQ, DP), BF),
            pltpu.VMEM((SEQ, FF), F32), pltpu.VMEM((SEQ, FF), F32), pltpu.VMEM((SEQ, FF), BF),
            pltpu.VMEM((SEQ, 2 * FF), BF), pltpu.VMEM((SEQ, DP), F32),
            pltpu.VMEM((SEQ, DP), BF), pltpu.VMEM((SEQ, DP), BF),
            pltpu.VMEM((HEADS, SEQ, SEQ), F32), pltpu.VMEM((HEADS, SEQ, SEQ), BF),
            pltpu.VMEM((SEQ, QK), F32), pltpu.VMEM((SEQ, QKVP), BF),
            pltpu.VMEM((SEQ, SEQ), F32), pltpu.VMEM((SEQ, SEQ), F32), pltpu.VMEM((8, DP), F32),
        ]
        + [pltpu.SemaphoreType.DMA((7,))]
        + [pltpu.SemaphoreType.DMA((n * N_AG,))] * 2
        + [pltpu.SemaphoreType.DMA((ns * N_RS,))] * 2
        + [pltpu.SemaphoreType.DMA((9,))] * 2
    )
    shape = jax.ShapeDtypeStruct
    hbm = pl.BlockSpec(memory_space=pl.ANY)
    passed = (shape(tokens.shape, BF), shape(tokens.shape, BF), shape((1, ROWS), F32), shape((1, ROWS), F32))
    out = pl.pallas_call(
        kernel,
        out_shape=passed + tuple(shape((32, cols), F32) for _, _, cols in SUMS),
        in_specs=[hbm, vmem, vmem, hbm, hbm, vmem, hbm, hbm, hbm, hbm, vmem],
        out_specs=(vmem,) * (4 + ns),
        scratch_shapes=scratch,
        compiler_params=pltpu.CompilerParams(
            collective_id=0, has_side_effects=True, vmem_limit_bytes=63 * 1024 * 1024
        ),
    )(
        tokens, segments, gain_attn, w_qkv[0], w_out[0], gain_ffn, w_gu[0], w_down[0], d_out,
        jnp.asarray(permutation(), BF), jnp.asarray(lane_frequencies(), F32),
    )
    acts, igrad, gga, ggf, gq, go, gg, gd = pl.pallas_call(
        lay_out,
        out_shape=passed + tuple(shape((ROWS, 1, cols), F32) for cols in (QKV, D, 2 * FF, FF)),
        in_specs=[vmem] * (4 + ns),
        out_specs=(vmem,) * 8,
    )(*out)
    gq, go, gg, gd = (jnp.swapaxes(g, 0, 1) for g in (gq, go, gg, gd))
    return acts[None], igrad[None], gga, gq, go, ggf, gg, gd


def solution(mesh):
    in_specs = (
        P(None, ("fsdp", "ctx"), None),
        P(None, "fsdp"),
        P("section", "fsdp"),
        P("section", "fsdp", None),
        P("section", "fsdp", None),
        P("section", "fsdp"),
        P("section", "fsdp", None),
        P("section", "fsdp", None),
        P(None, ("fsdp", "ctx"), None),
    )
    out_specs = (
        P("section", None, ("fsdp", "ctx"), None),
        P("section", None, ("fsdp", "ctx"), None),
        P("section", "fsdp"),
        P("section", "fsdp", None),
        P("section", "fsdp", None),
        P("section", "fsdp"),
        P("section", "fsdp", None),
        P("section", "fsdp", None),
    )
    return jax.shard_map(
        per_device, mesh=mesh, in_specs=in_specs, out_specs=out_specs, check_vma=False
    )
```
